32 devices in a mesh: groups: 2 (over y), gx: 8 (over z, x), gy: 2 (over core).
Axes of the slice: x: 2, y: 2, z: 4, core: 2. Of those that a mesh axis runs over, the one named last changes fastest.
Arguments:
- field: bfloat16 [16, 64, 64, 128], P(None, ('groups', 'gx'), 'gy'), parts along dimension 1, may hold values from -6 to 6
- cotangent: bfloat16 [16, 64, 64, 128], P(None, ('groups', 'gx'), 'gy'), parts along dimension 1, may hold values from -6 to 6
- spectral_weight: bfloat16 [2, 16, 16, 16384], P(None, None, None, ('gx', 'gy')), may hold values from -1 to 1
- point_weight: bfloat16 [16, 16], replicated, may hold values from -1.5 to 1.5
- bias: float32 [16], replicated, may hold values from -3 to 3
Outputs:
- layer_out: bfloat16 [16, 64, 64, 128], P(None, ('groups', 'gx'), 'gy'), parts along dimension 1
- field_grad: bfloat16 [16, 64, 64, 128], P(None, ('groups', 'gx'), 'gy'), parts along dimension 1
- weight_grad: float32 [4, 16, 16, 16384], P('groups', None, None, ('gx', 'gy')), parts along dimension 0
The draws below stay inside these ranges and needn't reach their ends.
There are 2 independent parts, one for each index of `groups`. The reference program is written for one: setup_inputs(seed, part) draws one part's arguments, and reference() takes and returns one part's arrays. A program takes and returns all parts, laid end to end along the dimension named above; an argument that names none is the same for every part. Nothing has to cross between parts.
All inputs are finite; a program needn't handle non-finite values.
Results may differ from the reference program's by a relative error of at most 0.0079.
Values may be sent and summed in bfloat16 or wider, within the bound.
A program may use at most 128 MiB of HBM per device.

```python
import math
import jax
import jax.numpy as jnp
from jax import lax

C = 16
MX = 32
MY = 32
MZ = 16
LX = 4
NZ = 128
NX = 32
NY = 64
MODES = 16384


def shard_levels(key, shape, pieces, least, high):
    loudness, own = 1.0, jax.random.fold_in(key, 6)
    for axis_at, parts in pieces:
        heights = jnp.exp(jax.random.uniform(jax.random.fold_in(own, axis_at), (parts,), jnp.float32, least / len(pieces), high / len(pieces)))
        loudness = loudness * jnp.repeat(heights, shape[axis_at] // parts).reshape([-1 if axis == axis_at else 1 for axis in range(len(shape))])
    return loudness


def normal_values(rng, dims, spread, most, shards=(), kind=jnp.bfloat16):
    loudness = shard_levels(rng, dims, shards, -0.22, 0.18) if shards else 1.0
    entries = jax.random.normal(rng, dims, jnp.float32) * spread * loudness
    return jnp.minimum(jnp.maximum(entries, -most), most).astype(kind)


def setup_inputs(seed: int = 0, part: int = 0) -> dict:
    splits = jax.random.split(jax.random.key(seed), 6)
    part_splits = jax.random.split(jax.random.fold_in(splits[5], part), 6)
    field = normal_values(part_splits[0], (C, NX, NY, NZ), 1.0, 6.0, ((1, 8), (2, 2)))
    cotangent = normal_values(part_splits[1], (C, NX, NY, NZ), 1.0, 6.0, ((1, 8), (2, 2)))
    spectral_weight = normal_values(splits[2], (2, C, C, MODES), (2 * C) ** -0.5, 1.0, ((3, 16),))
    point_weight = normal_values(splits[3], (C, C), C ** -0.5, 1.5)
    bias = normal_values(splits[4], (C,), 0.5, 3.0, (), jnp.float32)
    return {"field": field, "cotangent": cotangent, "spectral_weight": spectral_weight, "point_weight": point_weight, "bias": bias}


def phase_tables(count, length, offset, rows, signed):
    position = offset + jnp.arange(rows, dtype=jnp.int32)
    freq = jnp.arange(count, dtype=jnp.int32)
    if signed:
        freq = jnp.where(freq >= count // 2, freq + (length - count), freq)
    turns = freq[:, None] * position[None, :] % length
    angle = turns.astype(jnp.float32) * (2.0 * math.pi / length)
    return (jnp.cos(angle).astype(jnp.bfloat16), jnp.sin(angle).astype(jnp.bfloat16))

def z_transform(block, cos_z, sin_z):
    chans, rows_x, rows_y, nz_len = block.shape
    kept = cos_z.shape[0]
    tables = jnp.concatenate([cos_z, sin_z], axis=0)
    flat = jnp.dot(block.reshape(-1, nz_len), tables.T, preferred_element_type=jnp.float32)
    flat = flat.reshape(chans, rows_x, rows_y, 2 * kept)
    both = jnp.transpose(flat, (0, 3, 1, 2))
    return (both[:, :kept], both[:, kept:])

def point_mix(matrix, grid):
    chans = grid.shape[0]
    flat = jnp.dot(matrix, grid.reshape(chans, -1), preferred_element_type=jnp.float32)
    return flat.reshape(grid.shape)

def forward_yz(block, y_start, zscale, ny_total):
    hp = lax.Precision.HIGHEST
    rows_y = block.shape[2]
    nz_len = block.shape[3]
    cos_z, sin_z = phase_tables(MZ, nz_len, 0, nz_len, False)
    zscale_b = zscale[None, :, None, None]
    z_cos, z_sin = z_transform(block, cos_z, sin_z)
    part_r = z_cos * zscale_b
    part_i = -z_sin * zscale_b
    cos_y, sin_y = phase_tables(MY, ny_total, y_start, rows_y, True)
    cos_y = cos_y.astype(jnp.float32)
    sin_y = sin_y.astype(jnp.float32)
    out_r = jnp.einsum('ckxy,jy->cjkx', part_r, cos_y, precision=hp) + jnp.einsum('ckxy,jy->cjkx', part_i, sin_y, precision=hp)
    out_i = jnp.einsum('ckxy,jy->cjkx', part_i, cos_y, precision=hp) - jnp.einsum('ckxy,jy->cjkx', part_r, sin_y, precision=hp)
    return (out_r, out_i)

def forward_x(part_r, part_i, x_start, nx_total):
    hp = lax.Precision.HIGHEST
    chans = part_r.shape[0]
    rows_x = part_r.shape[3]
    cos_x, sin_x = phase_tables(MX, nx_total, x_start, rows_x, True)
    cos_x = cos_x.astype(jnp.float32)
    sin_x = sin_x.astype(jnp.float32)
    out_r = jnp.einsum('cjkx,ix->cjki', part_r, cos_x, precision=hp) + jnp.einsum('cjkx,ix->cjki', part_i, sin_x, precision=hp)
    out_i = jnp.einsum('cjkx,ix->cjki', part_i, cos_x, precision=hp) - jnp.einsum('cjkx,ix->cjki', part_r, sin_x, precision=hp)
    return jnp.stack([out_r.reshape(chans, -1), out_i.reshape(chans, -1)])

def inverse_modes(modes, x_start, y_start, zweight, nx_total, ny_total, rows_x, rows_y, nz_len):
    hp = lax.Precision.HIGHEST
    chans = modes.shape[1]
    values = modes.astype(jnp.float32).reshape(2, chans, MY, MZ, MX)
    mode_r = values[0]
    mode_i = values[1]
    cos_x, sin_x = phase_tables(MX, nx_total, x_start, rows_x, True)
    cos_x = cos_x.astype(jnp.float32)
    sin_x = sin_x.astype(jnp.float32)
    step_r = jnp.einsum('cjki,ix->cxjk', mode_r, cos_x, precision=hp) - jnp.einsum('cjki,ix->cxjk', mode_i, sin_x, precision=hp)
    step_i = jnp.einsum('cjki,ix->cxjk', mode_i, cos_x, precision=hp) + jnp.einsum('cjki,ix->cxjk', mode_r, sin_x, precision=hp)
    cos_y, sin_y = phase_tables(MY, ny_total, y_start, rows_y, True)
    cos_y = cos_y.astype(jnp.float32)
    sin_y = sin_y.astype(jnp.float32)
    next_r = jnp.einsum('cxjk,jy->cxyk', step_r, cos_y, precision=hp) - jnp.einsum('cxjk,jy->cxyk', step_i, sin_y, precision=hp)
    next_i = jnp.einsum('cxjk,jy->cxyk', step_i, cos_y, precision=hp) + jnp.einsum('cxjk,jy->cxyk', step_r, sin_y, precision=hp)
    cos_z, sin_z = phase_tables(MZ, nz_len, 0, nz_len, False)
    cos_z = cos_z.astype(jnp.float32)
    sin_z = sin_z.astype(jnp.float32)
    next_r = next_r * zweight
    next_i = next_i * zweight
    return jnp.einsum('cxyk,kz->cxyz', next_r, cos_z, precision=hp) - jnp.einsum('cxyk,kz->cxyz', next_i, sin_z, precision=hp)

def channel_mix(spectrum, weight):
    hp = lax.Precision.HIGHEST
    w_r = weight[0].astype(jnp.float32)
    w_i = weight[1].astype(jnp.float32)
    out_r = jnp.einsum('im,iom->om', spectrum[0], w_r, precision=hp) - jnp.einsum('im,iom->om', spectrum[1], w_i, precision=hp)
    out_i = jnp.einsum('im,iom->om', spectrum[1], w_r, precision=hp) + jnp.einsum('im,iom->om', spectrum[0], w_i, precision=hp)
    return jnp.stack([out_r, out_i])

def mix_grads(spectrum, mixed_grad, weight):
    hp = lax.Precision.HIGHEST
    w_r = weight[0].astype(jnp.float32)
    w_i = weight[1].astype(jnp.float32)
    grad_r = jnp.einsum('om,im->iom', mixed_grad[0], spectrum[0], precision=hp) + jnp.einsum('om,im->iom', mixed_grad[1], spectrum[1], precision=hp)
    grad_i = jnp.einsum('om,im->iom', mixed_grad[1], spectrum[0], precision=hp) - jnp.einsum('om,im->iom', mixed_grad[0], spectrum[1], precision=hp)
    back_r = jnp.einsum('iom,om->im', w_r, mixed_grad[0], precision=hp) + jnp.einsum('iom,om->im', w_i, mixed_grad[1], precision=hp)
    back_i = jnp.einsum('iom,om->im', w_r, mixed_grad[1], precision=hp) - jnp.einsum('iom,om->im', w_i, mixed_grad[0], precision=hp)
    return (jnp.stack([grad_r, grad_i]), jnp.stack([back_r, back_i]))

def reference(field, cotangent, spectral_weight, point_weight, bias):
    total_cells = NX * NY * NZ
    blocks = NX // LX
    zindex = jnp.arange(MZ, dtype=jnp.int32)
    forward_scale = jnp.full((MZ,), 1.0 / math.sqrt(total_cells), jnp.float32)
    inverse_scale = jnp.where(zindex == 0, 1.0, 2.0).astype(jnp.float32) / math.sqrt(2.0 * MODES)
    chans = field.shape[0]

    def forward_block(total, index):
        start = (index * LX).astype(jnp.int32)
        block = lax.dynamic_slice_in_dim(field, start, LX, 1)
        part_r, part_i = forward_yz(block, 0, forward_scale, NY)
        return (total + forward_x(part_r, part_i, start, NX), None)
    spectrum, _ = lax.scan(forward_block, jnp.zeros((2, chans, MODES), jnp.float32), jnp.arange(blocks, dtype=jnp.int32))
    mixed = channel_mix(spectrum, spectral_weight).astype(jnp.bfloat16)

    def middle_block(total, index):
        start = (index * LX).astype(jnp.int32)
        block = lax.dynamic_slice_in_dim(field, start, LX, 1)
        grad_block = lax.dynamic_slice_in_dim(cotangent, start, LX, 1)
        spectral_out = inverse_modes(mixed, start, 0, inverse_scale, NX, NY, LX, NY, NZ)
        pre = spectral_out + point_mix(point_weight.T, block) + bias[:, None, None, None]
        out_block = jax.nn.gelu(pre).astype(jnp.bfloat16)
        pre_grad = jax.vjp(jax.nn.gelu, pre)[1](grad_block.astype(jnp.float32))[0].astype(jnp.bfloat16)
        part_r, part_i = forward_yz(pre_grad, 0, inverse_scale, NY)
        return (total + forward_x(part_r, part_i, start, NX), (out_block, pre_grad))
    mixed_grad, (out_blocks, grad_blocks) = lax.scan(middle_block, jnp.zeros((2, chans, MODES), jnp.float32), jnp.arange(blocks, dtype=jnp.int32))
    weight_grad, spectrum_grad = mix_grads(spectrum, mixed_grad, spectral_weight)
    weight_grad = weight_grad * math.sqrt(2.0 * MODES / total_cells)
    spectrum_grad = spectrum_grad.astype(jnp.bfloat16)

    def backward_block(carry, inputs):
        index, pre_grad = inputs
        start = (index * LX).astype(jnp.int32)
        local = point_mix(point_weight, pre_grad)
        spectral = inverse_modes(spectrum_grad, start, 0, forward_scale, NX, NY, LX, NY, NZ)
        return (carry, (local + spectral).astype(jnp.bfloat16))
    _, field_blocks = lax.scan(backward_block, jnp.zeros((), jnp.float32), (jnp.arange(blocks, dtype=jnp.int32), grad_blocks))
    layer_out = jnp.transpose(out_blocks, (1, 0, 2, 3, 4)).reshape(chans, NX, NY, NZ)
    field_grad = jnp.transpose(field_blocks, (1, 0, 2, 3, 4)).reshape(chans, NX, NY, NZ)
    return (layer_out, field_grad, weight_grad)
```

```python
import math

import jax
import jax.numpy as jnp
import numpy as np
from jax import lax
from jax.experimental import pallas as pl
from jax.experimental.pallas import tpu as pltpu
from jax.sharding import PartitionSpec as P

MX = 32
MY = 32
MZ = 16


def phase_tables(count, length, offset, rows, signed):
    position = offset + jnp.arange(rows, dtype=jnp.int32)
    freq = jnp.arange(count, dtype=jnp.int32)
    if signed:
        freq = jnp.where(freq >= count // 2, freq + (length - count), freq)
    turns = freq[:, None] * position[None, :] % length
    angle = turns.astype(jnp.float32) * (2.0 * math.pi / length)
    return (jnp.cos(angle).astype(jnp.bfloat16), jnp.sin(angle).astype(jnp.bfloat16))


def z_transform(block, cos_z, sin_z):
    chans, rows_x, rows_y, nz_len = block.shape
    kept = cos_z.shape[0]
    tables = jnp.concatenate([cos_z, sin_z], axis=0)
    flat = jnp.dot(block.reshape(-1, nz_len), tables.T, preferred_element_type=jnp.float32)
    flat = flat.reshape(chans, rows_x, rows_y, 2 * kept)
    both = jnp.transpose(flat, (0, 3, 1, 2))
    return (both[:, :kept], both[:, kept:])


def point_mix(matrix, grid):
    chans = grid.shape[0]
    flat = jnp.dot(matrix, grid.reshape(chans, -1), preferred_element_type=jnp.float32)
    return flat.reshape(grid.shape)


def forward_yz(block, y_start, zscale, ny_total):
    hp = lax.Precision.HIGHEST
    rows_y = block.shape[2]
    nz_len = block.shape[3]
    cos_z, sin_z = phase_tables(MZ, nz_len, 0, nz_len, False)
    zscale_b = zscale[None, :, None, None]
    z_cos, z_sin = z_transform(block, cos_z, sin_z)
    part_r = z_cos * zscale_b
    part_i = -z_sin * zscale_b
    cos_y, sin_y = phase_tables(MY, ny_total, y_start, rows_y, True)
    cos_y = cos_y.astype(jnp.float32)
    sin_y = sin_y.astype(jnp.float32)
    out_r = jnp.einsum("ckxy,jy->cjkx", part_r, cos_y, precision=hp) + jnp.einsum(
        "ckxy,jy->cjkx", part_i, sin_y, precision=hp
    )
    out_i = jnp.einsum("ckxy,jy->cjkx", part_i, cos_y, precision=hp) - jnp.einsum(
        "ckxy,jy->cjkx", part_r, sin_y, precision=hp
    )
    return (out_r, out_i)


def forward_x(part_r, part_i, x_start, nx_total):
    hp = lax.Precision.HIGHEST
    chans = part_r.shape[0]
    rows_x = part_r.shape[3]
    cos_x, sin_x = phase_tables(MX, nx_total, x_start, rows_x, True)
    cos_x = cos_x.astype(jnp.float32)
    sin_x = sin_x.astype(jnp.float32)
    out_r = jnp.einsum("cjkx,ix->cjki", part_r, cos_x, precision=hp) + jnp.einsum(
        "cjkx,ix->cjki", part_i, sin_x, precision=hp
    )
    out_i = jnp.einsum("cjkx,ix->cjki", part_i, cos_x, precision=hp) - jnp.einsum(
        "cjkx,ix->cjki", part_r, sin_x, precision=hp
    )
    return jnp.stack([out_r.reshape(chans, -1), out_i.reshape(chans, -1)])


def inverse_modes(modes, x_start, y_start, zweight, nx_total, ny_total, rows_x, rows_y, nz_len):
    hp = lax.Precision.HIGHEST
    chans = modes.shape[1]
    values = modes.astype(jnp.float32).reshape(2, chans, MY, MZ, MX)
    mode_r = values[0]
    mode_i = values[1]
    cos_x, sin_x = phase_tables(MX, nx_total, x_start, rows_x, True)
    cos_x = cos_x.astype(jnp.float32)
    sin_x = sin_x.astype(jnp.float32)
    step_r = jnp.einsum("cjki,ix->cxjk", mode_r, cos_x, precision=hp) - jnp.einsum(
        "cjki,ix->cxjk", mode_i, sin_x, precision=hp
    )
    step_i = jnp.einsum("cjki,ix->cxjk", mode_i, cos_x, precision=hp) + jnp.einsum(
        "cjki,ix->cxjk", mode_r, sin_x, precision=hp
    )
    cos_y, sin_y = phase_tables(MY, ny_total, y_start, rows_y, True)
    cos_y = cos_y.astype(jnp.float32)
    sin_y = sin_y.astype(jnp.float32)
    next_r = jnp.einsum("cxjk,jy->cxyk", step_r, cos_y, precision=hp) - jnp.einsum(
        "cxjk,jy->cxyk", step_i, sin_y, precision=hp
    )
    next_i = jnp.einsum("cxjk,jy->cxyk", step_i, cos_y, precision=hp) + jnp.einsum(
        "cxjk,jy->cxyk", step_r, sin_y, precision=hp
    )
    cos_z, sin_z = phase_tables(MZ, nz_len, 0, nz_len, False)
    cos_z = cos_z.astype(jnp.float32)
    sin_z = sin_z.astype(jnp.float32)
    next_r = next_r * zweight
    next_i = next_i * zweight
    return jnp.einsum("cxyk,kz->cxyz", next_r, cos_z, precision=hp) - jnp.einsum(
        "cxyk,kz->cxyz", next_i, sin_z, precision=hp
    )


def channel_mix(spectrum, weight):
    hp = lax.Precision.HIGHEST
    w_r = weight[0].astype(jnp.float32)
    w_i = weight[1].astype(jnp.float32)
    out_r = jnp.einsum("im,iom->om", spectrum[0], w_r, precision=hp) - jnp.einsum(
        "im,iom->om", spectrum[1], w_i, precision=hp
    )
    out_i = jnp.einsum("im,iom->om", spectrum[1], w_r, precision=hp) + jnp.einsum(
        "im,iom->om", spectrum[0], w_i, precision=hp
    )
    return jnp.stack([out_r, out_i])


def mix_grads(spectrum, mixed_grad, weight):
    hp = lax.Precision.HIGHEST
    w_r = weight[0].astype(jnp.float32)
    w_i = weight[1].astype(jnp.float32)
    grad_r = jnp.einsum("om,im->iom", mixed_grad[0], spectrum[0], precision=hp) + jnp.einsum(
        "om,im->iom", mixed_grad[1], spectrum[1], precision=hp
    )
    grad_i = jnp.einsum("om,im->iom", mixed_grad[1], spectrum[0], precision=hp) - jnp.einsum(
        "om,im->iom", mixed_grad[0], spectrum[1], precision=hp
    )
    back_r = jnp.einsum("iom,om->im", w_r, mixed_grad[0], precision=hp) + jnp.einsum(
        "iom,om->im", w_i, mixed_grad[1], precision=hp
    )
    back_i = jnp.einsum("iom,om->im", w_r, mixed_grad[1], precision=hp) - jnp.einsum(
        "iom,om->im", w_i, mixed_grad[0], precision=hp
    )
    return (jnp.stack([grad_r, grad_i]), jnp.stack([back_r, back_i]))


def owned_spectrum(block, x_start, y_start, zscale, nx_total, ny_total):
    part_r, part_i = forward_yz(block, y_start, zscale, ny_total)
    whole = forward_x(part_r, part_i, x_start, nx_total)
    return lax.psum_scatter(whole, ("gx", "gy"), scatter_dimension=2, tiled=True)


def all_modes(owned_block):
    return lax.all_gather(owned_block, ("gx", "gy"), axis=2, tiled=True)


def on_device(field, cotangent, spectral_weight, point_weight, bias):
    rows_x = field.shape[1]
    rows_y = field.shape[2]
    nz_len = field.shape[3]
    nx_total = rows_x * lax.axis_size("gx")
    ny_total = rows_y * lax.axis_size("gy")
    total_cells = nx_total * ny_total * nz_len
    mode_count = MX * MY * MZ
    x_start = lax.axis_index("gx") * rows_x
    y_start = lax.axis_index("gy") * rows_y
    zindex = jnp.arange(MZ, dtype=jnp.int32)
    forward_scale = jnp.full((MZ,), 1.0 / math.sqrt(total_cells), jnp.float32)
    inverse_scale = jnp.where(zindex == 0, 1.0, 2.0).astype(jnp.float32) / math.sqrt(
        2.0 * mode_count
    )
    spectrum = owned_spectrum(field, x_start, y_start, forward_scale, nx_total, ny_total)
    mixed = channel_mix(spectrum, spectral_weight).astype(jnp.bfloat16)
    mixed_all = all_modes(mixed)
    spectral_out = inverse_modes(
        mixed_all, x_start, y_start, inverse_scale, nx_total, ny_total, rows_x, rows_y, nz_len
    )
    pre = spectral_out + point_mix(point_weight.T, field) + bias[:, None, None, None]
    layer_out = jax.nn.gelu(pre).astype(jnp.bfloat16)
    pre_grad = jax.vjp(jax.nn.gelu, pre)[1](cotangent.astype(jnp.float32))[0].astype(jnp.bfloat16)
    mixed_grad = owned_spectrum(pre_grad, x_start, y_start, inverse_scale, nx_total, ny_total)
    weight_grad, spectrum_grad = mix_grads(spectrum, mixed_grad, spectral_weight)
    weight_grad = weight_grad * math.sqrt(2.0 * mode_count / total_cells)
    grad_all = all_modes(spectrum_grad.astype(jnp.bfloat16))
    local = point_mix(point_weight, pre_grad)
    spectral = inverse_modes(
        grad_all, x_start, y_start, forward_scale, nx_total, ny_total, rows_x, rows_y, nz_len
    )
    field_grad = (local + spectral).astype(jnp.bfloat16)
    return (layer_out, field_grad, weight_grad)


BF = jnp.bfloat16
F32 = jnp.float32
MESH = pl.DeviceIdType.MESH
GC = 8


def host_tables(count, length, cells, signed):
    freq = np.arange(count)
    if signed:
        freq = np.where(freq >= count // 2, freq + (length - count), freq)
    turns = (freq[:, None] * cells[None, :]) % length
    angle = turns.astype(np.float32) * np.float32(2.0 * math.pi / length)
    rounded = [np.asarray(fn(angle)).astype(BF).astype(np.float32) for fn in (np.cos, np.sin)]
    return rounded[0], rounded[1]


def constant_tables(gx, gy, rows_x, rows_y, nz_len):
    nx_total, ny_total = rows_x * gx, rows_y * gy
    cos_x, sin_x = host_tables(MX, nx_total, np.arange(nx_total), True)
    cos_y, sin_y = host_tables(MY, ny_total, np.arange(ny_total), True)
    cos_z, sin_z = host_tables(MZ, nz_len, np.arange(nz_len), False)
    eye_c, eye_x, eye_k = np.eye(GC), np.eye(rows_x), np.eye(MZ)
    cy = cos_y.reshape(MY, gy, rows_y)
    sy = sin_y.reshape(MY, gy, rows_y)
    y_fwd = np.stack([np.einsum("jgy,cd->gjcdy", t, eye_c) for t in (cy, sy)], axis=1)
    y_fwd = y_fwd.reshape(gy, 2 * MY * GC, GC * rows_y)
    y_inv = np.stack([np.einsum("jgy,cd->gcyjd", t, eye_c) for t in (cy, -sy)], axis=3)
    y_inv = y_inv.reshape(gy, GC * rows_y, 2 * MY * GC)
    z_pairs = np.stack([np.stack([cos_z, -sin_z]), np.stack([-sin_z, -cos_z])])
    z_fwd = np.einsum("arkz,xw->axzrkw", z_pairs, eye_x)
    z_fwd = z_fwd.reshape(2 * rows_x * nz_len, 2 * MZ * rows_x)
    i_pairs = np.stack([np.stack([cos_z, -sin_z]), np.stack([sin_z, cos_z])])
    z_inv = np.einsum("arkz,xw->rkwaxz", i_pairs, eye_x)
    z_inv = z_inv.reshape(2 * MZ * rows_x, 2 * rows_x * nz_len)
    x_pairs = np.stack([np.stack([cos_x, -sin_x]), np.stack([sin_x, cos_x])])
    x_pairs = x_pairs.reshape(2, 2, MX, gx, rows_x)
    x_fwd = np.einsum("rsigx,kl->grkxsli", x_pairs, eye_k)
    x_fwd = x_fwd.reshape(gx * 2 * MZ * rows_x, 2 * MZ * MX)
    x_inv = np.ascontiguousarray(x_fwd.T)
    return [t.astype(BF) for t in (y_fwd, y_inv, z_fwd, z_inv, x_fwd, x_inv)]


def dot(a, b):
    return jnp.dot(a, b, preferred_element_type=F32)


def split_dot(a, b):
    high = a.astype(BF)
    low = (a - high.astype(F32)).astype(BF)
    both = dot(jnp.concatenate([high, low], axis=0), b)
    return both[: a.shape[0]] + both[a.shape[0] :]


def fused(
    gx, gy, zscales, inv_wg,
    field, cot, weight, point, bias, y_fwd, y_inv, z_fwd, z_inv, x_fwd, x_inv,
    layer_out, field_grad, weight_grad,
    send_a, send_b, recv, grid_f, grid_g, local, spec, grad, mode_grad, mix_a, mix_b, send_sem, recv_sem,
):
    peers = gx * gy
    chans, rows_x, rows_y, nz_len = field.shape
    half_rows = GC * rows_y
    halves = chans // GC
    slab = recv.shape[2]
    slab_half = slab // halves
    lanes = recv.shape[3]
    me_x, me_y = lax.axis_index("gx"), lax.axis_index("gy")
    me = me_x * gy + me_y
    half_modes = MZ * MX

    def peer(step):
        other = lax.rem(me + step, peers)
        return other, {"gx": other // gy, "gy": lax.rem(other, gy)}

    barrier = pltpu.get_barrier_semaphore()

    def greet(step, carry):
        pl.semaphore_signal(barrier, inc=1, device_id=peer(step)[1], device_id_type=MESH)
        return carry

    lax.fori_loop(1, peers, greet, 0)

    def copy_to(phase, buffer, step):
        other, where = peer(step)
        source = buffer.at[other] if buffer.shape[0] == peers else buffer.at[other // gy]
        return pltpu.make_async_remote_copy(
            src_ref=source,
            dst_ref=recv.at[phase, me],
            send_sem=send_sem.at[phase, other],
            recv_sem=recv_sem.at[phase, me],
            device_id=where,
            device_id_type=MESH,
        )

    def send(phase, buffer):
        def one(step, carry):
            copy_to(phase, buffer, step).start()
            return carry

        lax.fori_loop(1, peers, one, 0)
        own = buffer[me] if buffer.shape[0] == peers else buffer[me_x]
        recv[phase, me] = own

    def receive(phase, buffer):
        def one(step, carry):
            other, where = peer(step)
            pltpu.make_async_remote_copy(
                src_ref=recv.at[phase, other],
                dst_ref=recv.at[phase, other],
                send_sem=send_sem.at[phase, other],
                recv_sem=recv_sem.at[phase, other],
                device_id=where,
                device_id_type=MESH,
            ).wait_recv()
            return carry

        lax.fori_loop(1, peers, one, 0)

    def drain(phase, buffer):
        def one(step, carry):
            copy_to(phase, buffer, step).wait_send()
            return carry

        lax.fori_loop(1, peers, one, 0)

    def zweight(width, scale_zero, scale_rest):
        lane = lax.broadcasted_iota(jnp.int32, (1, width), 1)
        k = lax.rem(lane // rows_x, MZ)
        return jnp.where(k == 0, scale_zero, scale_rest).astype(F32)

    fwd_scale, inv_zero, inv_rest = zscales

    def to_modes(grid, buffer, scale):
        for h in range(halves):
            table = y_fwd[me_y]
            after_y = dot(table, grid[h * half_rows : (h + 1) * half_rows, :])
            rows = after_y.shape[0] // 2
            both = jnp.concatenate([after_y[:rows], after_y[rows:]], axis=1).astype(BF)
            out = (dot(both, z_fwd[...]) * scale).astype(BF)
            buffer[:, h * slab_half : (h + 1) * slab_half, :] = out.reshape(peers, slab_half, lanes)

    def owned(phase):
        parts = []
        for s in range(gx):
            total = recv[phase, s * gy].astype(F32)
            for t in range(1, gy):
                total = total + recv[phase, s * gy + t].astype(F32)
            parts.append(total)
        return split_dot(jnp.concatenate(parts, axis=1), x_fwd[...])

    def store_owned(values, store):
        for h in range(halves):
            for j in range(slab_half // GC):
                rows = values[h * slab_half + j * GC : h * slab_half + (j + 1) * GC]
                for r in range(2):
                    store[r, h * GC : (h + 1) * GC, j * half_modes : (j + 1) * half_modes] = rows[
                        :, r * half_modes : (r + 1) * half_modes
                    ]

    def to_slabs(store, buffer, scale):
        rows = []
        for h in range(halves):
            for j in range(slab_half // GC):
                rows.append(
                    jnp.concatenate(
                        [
                            store[r, h * GC : (h + 1) * GC, j * half_modes : (j + 1) * half_modes]
                            for r in range(2)
                        ],
                        axis=1,
                    )
                )
        values = jnp.concatenate(rows, axis=0).astype(BF)
        out = (dot(values, x_inv[...]) * scale).astype(BF)
        for s in range(gx):
            buffer[s] = out[:, s * lanes : (s + 1) * lanes]

    def to_grid(phase, h):
        modes = recv[phase, :, h * slab_half : (h + 1) * slab_half, :]
        modes = modes.reshape(peers * slab_half, lanes)
        after_z = dot(modes, z_inv[...]).astype(BF)
        width = rows_x * nz_len
        both = jnp.concatenate([after_z[:, :width], after_z[:, width:]], axis=0)
        return dot(y_inv[me_y], both)

    def spread(matrix):
        n = chans * rows_y
        row = lax.broadcasted_iota(jnp.int32, (n, chans), 0) // rows_y
        pick = (row == lax.broadcasted_iota(jnp.int32, (n, chans), 1)).astype(BF)
        col = lax.broadcasted_iota(jnp.int32, (chans, n), 1) // rows_y
        pick_t = (col == lax.broadcasted_iota(jnp.int32, (chans, n), 0)).astype(BF)
        wide = dot(dot(pick, matrix).astype(BF), pick_t)
        diag = lax.rem(lax.broadcasted_iota(jnp.int32, (n, n), 0), rows_y) == lax.rem(
            lax.broadcasted_iota(jnp.int32, (n, n), 1), rows_y
        )
        return jnp.where(diag, wide, 0.0).astype(BF)

    for c in range(chans):
        for x in range(rows_x):
            grid_f[c * rows_y : (c + 1) * rows_y, x * nz_len : (x + 1) * nz_len] = field[c, x]
    to_modes(grid_f, send_a.at[0], fwd_scale)
    pl.semaphore_wait(barrier, peers - 1)
    send(0, send_a.at[0])
    mix_a[...] = spread(point[...].T)
    mix_b[...] = spread(point[...])
    local[...] = dot(mix_a[...], grid_f[...])
    receive(0, send_a.at[0])

    store_owned(owned(0), spec)
    half = half_modes
    for j in range(slab_half // GC):
        span = slice(j * half, (j + 1) * half)
        mixed_r = jnp.zeros((chans, half), F32)
        mixed_i = jnp.zeros((chans, half), F32)
        for c in range(chans):
            w_r = weight[0, c, :, span].astype(F32)
            w_i = weight[1, c, :, span].astype(F32)
            s_r = spec[0, c : c + 1, span]
            s_i = spec[1, c : c + 1, span]
            mixed_r = mixed_r + (s_r * w_r - s_i * w_i)
            mixed_i = mixed_i + (s_i * w_r + s_r * w_i)
        grad[0, :, span] = mixed_r
        grad[1, :, span] = mixed_i
    to_slabs(grad, send_b.at[0], zweight(gx * lanes, inv_zero, inv_rest))
    send(1, send_b.at[0])
    receive(1, send_b.at[0])

    a = math.sqrt(2.0 / math.pi)
    for h in range(halves):
        rows = slice(h * half_rows, (h + 1) * half_rows)
        pre_half = to_grid(1, h) + local[rows, :]
        for c in range(GC):
            o = h * GC + c
            pre = pre_half[c * rows_y : (c + 1) * rows_y] + bias[o]
            square = pre * pre
            t = jnp.tanh(a * pre * (1.0 + 0.044715 * square))
            cdf = 0.5 * (1.0 + t)
            out = (pre * cdf).astype(BF)
            slope = cdf + 0.5 * pre * (1.0 - t * t) * (a * (1.0 + 3.0 * 0.044715 * square))
            for x in range(rows_x):
                cols = slice(x * nz_len, (x + 1) * nz_len)
                layer_out[o, x] = out[:, cols]
                grid_g[o * rows_y : (o + 1) * rows_y, cols] = (
                    cot[o, x].astype(F32) * slope[:, cols]
                ).astype(BF)
    to_modes(grid_g, send_a.at[1], zweight(lanes, inv_zero, inv_rest))
    send(2, send_a.at[1])
    local[...] = dot(mix_b[...], grid_g[...])
    receive(2, send_a.at[1])

    store_owned(owned(2), grad)
    for j in range(slab_half // GC):
        span = slice(j * half, (j + 1) * half)
        g_r = grad[0, :, span]
        g_i = grad[1, :, span]
        for c in range(chans):
            w_r = weight[0, c, :, span].astype(F32)
            w_i = weight[1, c, :, span].astype(F32)
            mode_grad[0, c : c + 1, span] = jnp.sum(w_r * g_r + w_i * g_i, axis=0, keepdims=True)
            mode_grad[1, c : c + 1, span] = jnp.sum(w_r * g_i - w_i * g_r, axis=0, keepdims=True)
    to_slabs(mode_grad, send_b.at[1], fwd_scale)
    send(3, send_b.at[1])
    for j in range(slab_half // GC):
        span = slice(j * half, (j + 1) * half)
        g_r = grad[0, :, span] * inv_wg
        g_i = grad[1, :, span] * inv_wg
        for c in range(chans):
            s_r = spec[0, c : c + 1, span]
            s_i = spec[1, c : c + 1, span]
            weight_grad[0, c, :, span] = g_r * s_r + g_i * s_i
            weight_grad[1, c, :, span] = g_i * s_r - g_r * s_i
    receive(3, send_b.at[1])
    for h in range(halves):
        total = to_grid(3, h) + local[h * half_rows : (h + 1) * half_rows, :]
        out = total.astype(BF)
        for c in range(GC):
            for x in range(rows_x):
                field_grad[h * GC + c, x] = out[
                    c * rows_y : (c + 1) * rows_y, x * nz_len : (x + 1) * nz_len
                ]
    drain(0, send_a.at[0])
    drain(1, send_b.at[0])
    drain(2, send_a.at[1])
    drain(3, send_b.at[1])


def on_device_fused(gx, gy, field, cotangent, spectral_weight, point_weight, bias):
    chans, rows_x, rows_y, nz_len = field.shape
    peers = gx * gy
    owned_modes = spectral_weight.shape[3]
    total_cells = gx * gy * rows_x * rows_y * nz_len
    mode_count = MX * MY * MZ
    inv = 1.0 / math.sqrt(2.0 * mode_count)
    zscales = (1.0 / math.sqrt(total_cells), inv, 2.0 * inv)
    wg_scale = math.sqrt(2.0 * mode_count / total_cells)
    tables = [jnp.asarray(t) for t in constant_tables(gx, gy, rows_x, rows_y, nz_len)]
    slab = MY // peers * chans
    lanes = 2 * MZ * rows_x
    rows, width = chans * rows_y, rows_x * nz_len
    vmem = pl.BlockSpec(memory_space=pltpu.VMEM)
    smem = pl.BlockSpec(memory_space=pltpu.SMEM)

    def body(*refs):
        fused(gx, gy, zscales, wg_scale, *refs)

    return pl.pallas_call(
        body,
        out_shape=(
            jax.ShapeDtypeStruct(field.shape, BF),
            jax.ShapeDtypeStruct(field.shape, BF),
            jax.ShapeDtypeStruct(spectral_weight.shape, F32),
        ),
        in_specs=[vmem, vmem, vmem, vmem, smem] + [vmem] * 6,
        out_specs=(vmem, vmem, vmem),
        scratch_shapes=[
            pltpu.VMEM((2, peers, slab, lanes), BF),
            pltpu.VMEM((2, gx, slab, lanes), BF),
            pltpu.VMEM((4, peers, slab, lanes), BF),
            pltpu.VMEM((rows, width), BF),
            pltpu.VMEM((rows, width), BF),
            pltpu.VMEM((rows, width), F32),
            pltpu.VMEM((2, chans, owned_modes), F32),
            pltpu.VMEM((2, chans, owned_modes), F32),
            pltpu.VMEM((2, chans, owned_modes), F32),
            pltpu.VMEM((rows, rows), BF),
            pltpu.VMEM((rows, rows), BF),
            pltpu.SemaphoreType.DMA((4, peers)),
            pltpu.SemaphoreType.DMA((4, peers)),
        ],
        compiler_params=pltpu.CompilerParams(
            collective_id=0, has_side_effects=True, vmem_limit_bytes=48 * 1024 * 1024
        ),
    )(field, cotangent, spectral_weight, point_weight, bias, *tables)


def solution(mesh):
    gx, gy = mesh.shape["gx"], mesh.shape["gy"]
    in_specs = (
        P(None, ("groups", "gx"), "gy", None),
        P(None, ("groups", "gx"), "gy", None),
        P(None, None, None, ("gx", "gy")),
        P(),
        P(),
    )
    out_specs = (
        P(None, ("groups", "gx"), "gy", None),
        P(None, ("groups", "gx"), "gy", None),
        P("groups", None, None, ("gx", "gy")),
    )

    def local_program(field, cotangent, spectral_weight, point_weight, bias):
        rows_x = field.shape[1]
        fits = MY % (gx * gy) == 0 and MY // (gx * gy) * GC % 16 == 0
        fits = fits and 2 * MZ * rows_x == 128 and field.shape[0] % GC == 0
        if fits:
            return on_device_fused(gx, gy, field, cotangent, spectral_weight, point_weight, bias)
        return on_device(field, cotangent, spectral_weight, point_weight, bias)

    return jax.shard_map(
        local_program, mesh=mesh, in_specs=in_specs, out_specs=out_specs, check_vma=False
    )
```

```python
import math

import jax
import jax.numpy as jnp
import numpy as np
from jax import lax
from jax.experimental import pallas as pl
from jax.experimental.pallas import tpu as pltpu
from jax.sharding import PartitionSpec as P

MX = 32
MY = 32
MZ = 16


def phase_tables(count, length, offset, rows, signed):
    position = offset + jnp.arange(rows, dtype=jnp.int32)
    freq = jnp.arange(count, dtype=jnp.int32)
    if signed:
        freq = jnp.where(freq >= count // 2, freq + (length - count), freq)
    turns = freq[:, None] * position[None, :] % length
    angle = turns.astype(jnp.float32) * (2.0 * math.pi / length)
    return (jnp.cos(angle).astype(jnp.bfloat16), jnp.sin(angle).astype(jnp.bfloat16))


def z_transform(block, cos_z, sin_z):
    chans, rows_x, rows_y, nz_len = block.shape
    kept = cos_z.shape[0]
    tables = jnp.concatenate([cos_z, sin_z], axis=0)
    flat = jnp.dot(block.reshape(-1, nz_len), tables.T, preferred_element_type=jnp.float32)
    flat = flat.reshape(chans, rows_x, rows_y, 2 * kept)
    both = jnp.transpose(flat, (0, 3, 1, 2))
    return (both[:, :kept], both[:, kept:])


def point_mix(matrix, grid):
    chans = grid.shape[0]
    flat = jnp.dot(matrix, grid.reshape(chans, -1), preferred_element_type=jnp.float32)
    return flat.reshape(grid.shape)


def forward_yz(block, y_start, zscale, ny_total):
    hp = lax.Precision.HIGHEST
    rows_y = block.shape[2]
    nz_len = block.shape[3]
    cos_z, sin_z = phase_tables(MZ, nz_len, 0, nz_len, False)
    zscale_b = zscale[None, :, None, None]
    z_cos, z_sin = z_transform(block, cos_z, sin_z)
    part_r = z_cos * zscale_b
    part_i = -z_sin * zscale_b
    cos_y, sin_y = phase_tables(MY, ny_total, y_start, rows_y, True)
    cos_y = cos_y.astype(jnp.float32)
    sin_y = sin_y.astype(jnp.float32)
    out_r = jnp.einsum("ckxy,jy->cjkx", part_r, cos_y, precision=hp) + jnp.einsum(
        "ckxy,jy->cjkx", part_i, sin_y, precision=hp
    )
    out_i = jnp.einsum("ckxy,jy->cjkx", part_i, cos_y, precision=hp) - jnp.einsum(
        "ckxy,jy->cjkx", part_r, sin_y, precision=hp
    )
    return (out_r, out_i)


def forward_x(part_r, part_i, x_start, nx_total):
    hp = lax.Precision.HIGHEST
    chans = part_r.shape[0]
    rows_x = part_r.shape[3]
    cos_x, sin_x = phase_tables(MX, nx_total, x_start, rows_x, True)
    cos_x = cos_x.astype(jnp.float32)
    sin_x = sin_x.astype(jnp.float32)
    out_r = jnp.einsum("cjkx,ix->cjki", part_r, cos_x, precision=hp) + jnp.einsum(
        "cjkx,ix->cjki", part_i, sin_x, precision=hp
    )
    out_i = jnp.einsum("cjkx,ix->cjki", part_i, cos_x, precision=hp) - jnp.einsum(
        "cjkx,ix->cjki", part_r, sin_x, precision=hp
    )
    return jnp.stack([out_r.reshape(chans, -1), out_i.reshape(chans, -1)])


def inverse_modes(modes, x_start, y_start, zweight, nx_total, ny_total, rows_x, rows_y, nz_len):
    hp = lax.Precision.HIGHEST
    chans = modes.shape[1]
    values = modes.astype(jnp.float32).reshape(2, chans, MY, MZ, MX)
    mode_r = values[0]
    mode_i = values[1]
    cos_x, sin_x = phase_tables(MX, nx_total, x_start, rows_x, True)
    cos_x = cos_x.astype(jnp.float32)
    sin_x = sin_x.astype(jnp.float32)
    step_r = jnp.einsum("cjki,ix->cxjk", mode_r, cos_x, precision=hp) - jnp.einsum(
        "cjki,ix->cxjk", mode_i, sin_x, precision=hp
    )
    step_i = jnp.einsum("cjki,ix->cxjk", mode_i, cos_x, precision=hp) + jnp.einsum(
        "cjki,ix->cxjk", mode_r, sin_x, precision=hp
    )
    cos_y, sin_y = phase_tables(MY, ny_total, y_start, rows_y, True)
    cos_y = cos_y.astype(jnp.float32)
    sin_y = sin_y.astype(jnp.float32)
    next_r = jnp.einsum("cxjk,jy->cxyk", step_r, cos_y, precision=hp) - jnp.einsum(
        "cxjk,jy->cxyk", step_i, sin_y, precision=hp
    )
    next_i = jnp.einsum("cxjk,jy->cxyk", step_i, cos_y, precision=hp) + jnp.einsum(
        "cxjk,jy->cxyk", step_r, sin_y, precision=hp
    )
    cos_z, sin_z = phase_tables(MZ, nz_len, 0, nz_len, False)
    cos_z = cos_z.astype(jnp.float32)
    sin_z = sin_z.astype(jnp.float32)
    next_r = next_r * zweight
    next_i = next_i * zweight
    return jnp.einsum("cxyk,kz->cxyz", next_r, cos_z, precision=hp) - jnp.einsum(
        "cxyk,kz->cxyz", next_i, sin_z, precision=hp
    )


def channel_mix(spectrum, weight):
    hp = lax.Precision.HIGHEST
    w_r = weight[0].astype(jnp.float32)
    w_i = weight[1].astype(jnp.float32)
    out_r = jnp.einsum("im,iom->om", spectrum[0], w_r, precision=hp) - jnp.einsum(
        "im,iom->om", spectrum[1], w_i, precision=hp
    )
    out_i = jnp.einsum("im,iom->om", spectrum[1], w_r, precision=hp) + jnp.einsum(
        "im,iom->om", spectrum[0], w_i, precision=hp
    )
    return jnp.stack([out_r, out_i])


def mix_grads(spectrum, mixed_grad, weight):
    hp = lax.Precision.HIGHEST
    w_r = weight[0].astype(jnp.float32)
    w_i = weight[1].astype(jnp.float32)
    grad_r = jnp.einsum("om,im->iom", mixed_grad[0], spectrum[0], precision=hp) + jnp.einsum(
        "om,im->iom", mixed_grad[1], spectrum[1], precision=hp
    )
    grad_i = jnp.einsum("om,im->iom", mixed_grad[1], spectrum[0], precision=hp) - jnp.einsum(
        "om,im->iom", mixed_grad[0], spectrum[1], precision=hp
    )
    back_r = jnp.einsum("iom,om->im", w_r, mixed_grad[0], precision=hp) + jnp.einsum(
        "iom,om->im", w_i, mixed_grad[1], precision=hp
    )
    back_i = jnp.einsum("iom,om->im", w_r, mixed_grad[1], precision=hp) - jnp.einsum(
        "iom,om->im", w_i, mixed_grad[0], precision=hp
    )
    return (jnp.stack([grad_r, grad_i]), jnp.stack([back_r, back_i]))


def owned_spectrum(block, x_start, y_start, zscale, nx_total, ny_total):
    part_r, part_i = forward_yz(block, y_start, zscale, ny_total)
    whole = forward_x(part_r, part_i, x_start, nx_total)
    return lax.psum_scatter(whole, ("gx", "gy"), scatter_dimension=2, tiled=True)


def all_modes(owned_block):
    return lax.all_gather(owned_block, ("gx", "gy"), axis=2, tiled=True)


def on_device(field, cotangent, spectral_weight, point_weight, bias):
    rows_x = field.shape[1]
    rows_y = field.shape[2]
    nz_len = field.shape[3]
    nx_total = rows_x * lax.axis_size("gx")
    ny_total = rows_y * lax.axis_size("gy")
    total_cells = nx_total * ny_total * nz_len
    mode_count = MX * MY * MZ
    x_start = lax.axis_index("gx") * rows_x
    y_start = lax.axis_index("gy") * rows_y
    zindex = jnp.arange(MZ, dtype=jnp.int32)
    forward_scale = jnp.full((MZ,), 1.0 / math.sqrt(total_cells), jnp.float32)
    inverse_scale = jnp.where(zindex == 0, 1.0, 2.0).astype(jnp.float32) / math.sqrt(
        2.0 * mode_count
    )
    spectrum = owned_spectrum(field, x_start, y_start, forward_scale, nx_total, ny_total)
    mixed = channel_mix(spectrum, spectral_weight).astype(jnp.bfloat16)
    mixed_all = all_modes(mixed)
    spectral_out = inverse_modes(
        mixed_all, x_start, y_start, inverse_scale, nx_total, ny_total, rows_x, rows_y, nz_len
    )
    pre = spectral_out + point_mix(point_weight.T, field) + bias[:, None, None, None]
    layer_out = jax.nn.gelu(pre).astype(jnp.bfloat16)
    pre_grad = jax.vjp(jax.nn.gelu, pre)[1](cotangent.astype(jnp.float32))[0].astype(jnp.bfloat16)
    mixed_grad = owned_spectrum(pre_grad, x_start, y_start, inverse_scale, nx_total, ny_total)
    weight_grad, spectrum_grad = mix_grads(spectrum, mixed_grad, spectral_weight)
    weight_grad = weight_grad * math.sqrt(2.0 * mode_count / total_cells)
    grad_all = all_modes(spectrum_grad.astype(jnp.bfloat16))
    local = point_mix(point_weight, pre_grad)
    spectral = inverse_modes(
        grad_all, x_start, y_start, forward_scale, nx_total, ny_total, rows_x, rows_y, nz_len
    )
    field_grad = (local + spectral).astype(jnp.bfloat16)
    return (layer_out, field_grad, weight_grad)


BF = jnp.bfloat16
F32 = jnp.float32
MESH = pl.DeviceIdType.MESH
GC = 8


def host_tables(count, length, cells, signed):
    freq = np.arange(count)
    if signed:
        freq = np.where(freq >= count // 2, freq + (length - count), freq)
    turns = (freq[:, None] * cells[None, :]) % length
    angle = turns.astype(np.float32) * np.float32(2.0 * math.pi / length)
    rounded = [np.asarray(fn(angle)).astype(BF).astype(np.float32) for fn in (np.cos, np.sin)]
    return rounded[0], rounded[1]


def constant_tables(gx, gy, rows_x, rows_y, nz_len):
    nx_total, ny_total = rows_x * gx, rows_y * gy
    cos_x, sin_x = host_tables(MX, nx_total, np.arange(nx_total), True)
    cos_y, sin_y = host_tables(MY, ny_total, np.arange(ny_total), True)
    cos_z, sin_z = host_tables(MZ, nz_len, np.arange(nz_len), False)
    eye_c, eye_x, eye_k = np.eye(GC), np.eye(rows_x), np.eye(MZ)
    cy = cos_y.reshape(MY, gy, rows_y)
    sy = sin_y.reshape(MY, gy, rows_y)
    y_fwd = np.stack([np.einsum("jgy,cd->gjcdy", t, eye_c) for t in (cy, sy)], axis=1)
    y_fwd = y_fwd.reshape(gy, 2 * MY * GC, GC * rows_y)
    y_inv = np.stack([np.einsum("jgy,cd->gcyjd", t, eye_c) for t in (cy, -sy)], axis=3)
    y_inv = y_inv.reshape(gy, GC * rows_y, 2 * MY * GC)
    z_pairs = np.stack([np.stack([cos_z, -sin_z]), np.stack([-sin_z, -cos_z])])
    z_fwd = np.einsum("arkz,xw->axzrkw", z_pairs, eye_x)
    z_fwd = z_fwd.reshape(2 * rows_x * nz_len, 2 * MZ * rows_x)
    i_pairs = np.stack([np.stack([cos_z, -sin_z]), np.stack([sin_z, cos_z])])
    z_inv = np.einsum("arkz,xw->rkwaxz", i_pairs, eye_x)
    z_inv = z_inv.reshape(2 * MZ * rows_x, 2 * rows_x * nz_len)
    x_pairs = np.stack([np.stack([cos_x, -sin_x]), np.stack([sin_x, cos_x])])
    x_pairs = x_pairs.reshape(2, 2, MX, gx, rows_x)
    x_fwd = np.einsum("rsigx,kl->grkxsli", x_pairs, eye_k)
    x_fwd = x_fwd.reshape(gx * 2 * MZ * rows_x, 2 * MZ * MX)
    x_inv = np.ascontiguousarray(x_fwd.T)
    return [t.astype(BF) for t in (y_fwd, y_inv, z_fwd, z_inv, x_fwd, x_inv)]


def dot(a, b):
    return jnp.dot(a, b, preferred_element_type=F32)


def split_dot(a, b):
    high = a.astype(BF)
    low = (a - high.astype(F32)).astype(BF)
    both = dot(jnp.concatenate([high, low], axis=0), b)
    return both[: a.shape[0]] + both[a.shape[0] :]


def fused(
    gx, gy, zscales, inv_wg,
    field_h, cot_h, weight_h, point, bias, y_fwd_h, y_inv_h, z_fwd_h, z_inv_h, x_fwd_h, x_inv_h,
    layer_out_h, field_grad_h, weight_grad_h,
    field, cot, weight, y_fwd, y_inv, z_fwd, z_inv, x_fwd, x_inv, layer_out, field_grad, weight_grad,
    send_a, send_b, recv, grid_g, local, spec, grad, mode_grad, mix_a, mix_b, send_sem, recv_sem,
    load_sem, store_sem,
):
    peers = gx * gy
    chans, rows_x, rows_y, nz_len = field_h.shape
    half_rows = GC * rows_y
    halves = chans // GC
    slab = recv.shape[2]
    slab_half = slab // halves
    lanes = recv.shape[3]
    me_x, me_y = lax.axis_index("gx"), lax.axis_index("gy")
    me = me_x * gy + me_y
    half_modes = MZ * MX

    def peer(step):
        other = lax.rem(me + step, peers)
        return other, {"gx": other // gy, "gy": lax.rem(other, gy)}

    barrier = pltpu.get_barrier_semaphore()
    loads = {}

    def load(name, *pairs):
        copies = []
        for source, target in pairs:
            count = sum(len(c) for c in loads.values()) + len(copies)
            copies.append(pltpu.make_async_copy(source, target, load_sem.at[count]))
            copies[-1].start()
        loads[name] = copies

    def loaded(*names):
        for name in names:
            for copy in loads[name]:
                copy.wait()

    def by_x(flat, grid):
        return [
            (flat.at[:, x], grid.at[:, :, x * nz_len : (x + 1) * nz_len]) for x in range(rows_x)
        ]

    load("field", *by_x(field_h, field))
    load("y_fwd", (y_fwd_h.at[me_y], y_fwd))
    load("z_fwd", (z_fwd_h, z_fwd))
    load("x_fwd", (x_fwd_h, x_fwd))
    load("weight", (weight_h, weight))
    load("x_inv", (x_inv_h, x_inv))
    load("z_inv", (z_inv_h, z_inv))
    load("y_inv", (y_inv_h.at[me_y], y_inv))
    load("cot", *by_x(cot_h, cot))

    def greet(step, carry):
        pl.semaphore_signal(barrier, inc=1, device_id=peer(step)[1], device_id_type=MESH)
        return carry

    lax.fori_loop(1, peers, greet, 0)

    def copy_to(phase, buffer, step):
        other, where = peer(step)
        source = buffer.at[other] if buffer.shape[0] == peers else buffer.at[other // gy]
        return pltpu.make_async_remote_copy(
            src_ref=source,
            dst_ref=recv.at[phase, me],
            send_sem=send_sem.at[phase, other],
            recv_sem=recv_sem.at[phase, me],
            device_id=where,
            device_id_type=MESH,
        )

    def send(phase, buffer):
        def one(step, carry):
            copy_to(phase, buffer, step).start()
            return carry

        lax.fori_loop(1, peers, one, 0)
        own = buffer[me] if buffer.shape[0] == peers else buffer[me_x]
        recv[phase, me] = own

    def receive(phase, buffer):
        def one(step, carry):
            other, where = peer(step)
            pltpu.make_async_remote_copy(
                src_ref=recv.at[phase, other],
                dst_ref=recv.at[phase, other],
                send_sem=send_sem.at[phase, other],
                recv_sem=recv_sem.at[phase, other],
                device_id=where,
                device_id_type=MESH,
            ).wait_recv()
            return carry

        lax.fori_loop(1, peers, one, 0)

    def drain(phase, buffer):
        def one(step, carry):
            copy_to(phase, buffer, step).wait_send()
            return carry

        lax.fori_loop(1, peers, one, 0)

    def zweight(width, scale_zero, scale_rest):
        lane = lax.broadcasted_iota(jnp.int32, (1, width), 1)
        k = lax.rem(lane // rows_x, MZ)
        return jnp.where(k == 0, scale_zero, scale_rest).astype(F32)

    fwd_scale, inv_zero, inv_rest = zscales

    width = rows_x * nz_len

    def grid_half(grid, h):
        return grid[h * GC : (h + 1) * GC].reshape(half_rows, width)

    def whole(grid):
        return grid[...].reshape(chans * rows_y, width)

    def to_modes(grid, buffer, scale):
        for h in range(halves):
            after_y = dot(y_fwd[...], grid_half(grid, h))
            rows = after_y.shape[0] // 2
            both = jnp.concatenate([after_y[:rows], after_y[rows:]], axis=1).astype(BF)
            out = (dot(both, z_fwd[...]) * scale).astype(BF)
            buffer[:, h * slab_half : (h + 1) * slab_half, :] = out.reshape(peers, slab_half, lanes)

    def owned(phase):
        parts = []
        for s in range(gx):
            total = recv[phase, s * gy].astype(F32)
            for t in range(1, gy):
                total = total + recv[phase, s * gy + t].astype(F32)
            parts.append(total)
        return split_dot(jnp.concatenate(parts, axis=1), x_fwd[...])

    def store_owned(values, store):
        for h in range(halves):
            for j in range(slab_half // GC):
                rows = values[h * slab_half + j * GC : h * slab_half + (j + 1) * GC]
                for r in range(2):
                    store[r, h * GC : (h + 1) * GC, j * half_modes : (j + 1) * half_modes] = rows[
                        :, r * half_modes : (r + 1) * half_modes
                    ]

    def to_slabs(store, buffer, scale):
        rows = []
        for h in range(halves):
            for j in range(slab_half // GC):
                rows.append(
                    jnp.concatenate(
                        [
                            store[r, h * GC : (h + 1) * GC, j * half_modes : (j + 1) * half_modes]
                            for r in range(2)
                        ],
                        axis=1,
                    )
                )
        values = jnp.concatenate(rows, axis=0).astype(BF)
        out = (dot(values, x_inv[...]) * scale).astype(BF)
        for s in range(gx):
            buffer[s] = out[:, s * lanes : (s + 1) * lanes]

    def to_grid(phase, h):
        modes = recv[phase, :, h * slab_half : (h + 1) * slab_half, :]
        modes = modes.reshape(peers * slab_half, lanes)
        after_z = dot(modes, z_inv[...]).astype(BF)
        both = jnp.concatenate([after_z[:, :width], after_z[:, width:]], axis=0)
        return dot(y_inv[...], both)

    def spread(matrix):
        n = chans * rows_y
        row = lax.broadcasted_iota(jnp.int32, (n, chans), 0) // rows_y
        pick = (row == lax.broadcasted_iota(jnp.int32, (n, chans), 1)).astype(BF)
        col = lax.broadcasted_iota(jnp.int32, (chans, n), 1) // rows_y
        pick_t = (col == lax.broadcasted_iota(jnp.int32, (chans, n), 0)).astype(BF)
        wide = dot(dot(pick, matrix).astype(BF), pick_t)
        diag = lax.rem(lax.broadcasted_iota(jnp.int32, (n, n), 0), rows_y) == lax.rem(
            lax.broadcasted_iota(jnp.int32, (n, n), 1), rows_y
        )
        return jnp.where(diag, wide, 0.0).astype(BF)

    loaded("field", "y_fwd", "z_fwd")
    to_modes(field, send_a.at[0], fwd_scale)
    pl.semaphore_wait(barrier, peers - 1)
    send(0, send_a.at[0])
    mix_a[...] = spread(point[...].T)
    mix_b[...] = spread(point[...])
    local[...] = dot(mix_a[...], whole(field))
    receive(0, send_a.at[0])

    loaded("x_fwd")
    store_owned(owned(0), spec)
    loaded("weight", "x_inv")
    half = half_modes
    for j in range(slab_half // GC):
        span = slice(j * half, (j + 1) * half)
        mixed_r = jnp.zeros((chans, half), F32)
        mixed_i = jnp.zeros((chans, half), F32)
        for c in range(chans):
            w_r = weight[0, c, :, span].astype(F32)
            w_i = weight[1, c, :, span].astype(F32)
            s_r = spec[0, c : c + 1, span]
            s_i = spec[1, c : c + 1, span]
            mixed_r = mixed_r + (s_r * w_r - s_i * w_i)
            mixed_i = mixed_i + (s_i * w_r + s_r * w_i)
        grad[0, :, span] = mixed_r
        grad[1, :, span] = mixed_i
    to_slabs(grad, send_b.at[0], zweight(gx * lanes, inv_zero, inv_rest))
    send(1, send_b.at[0])
    receive(1, send_b.at[0])

    loaded("z_inv", "y_inv", "cot")
    a = math.sqrt(2.0 / math.pi)
    for h in range(halves):
        rows = slice(h * half_rows, (h + 1) * half_rows)
        pre_half = to_grid(1, h) + local[rows, :]
        for c in range(GC):
            o = h * GC + c
            pre = pre_half[c * rows_y : (c + 1) * rows_y] + bias[o]
            square = pre * pre
            t = jnp.tanh(a * pre * (1.0 + 0.044715 * square))
            cdf = 0.5 * (1.0 + t)
            out = (pre * cdf).astype(BF)
            slope = cdf + 0.5 * pre * (1.0 - t * t) * (a * (1.0 + 3.0 * 0.044715 * square))
            layer_out[o] = out
            grid_g[o] = (cot[o].astype(F32) * slope).astype(BF)
    stores = [
        pltpu.make_async_copy(s, d, store_sem.at[n])
        for n, (d, s) in enumerate(by_x(layer_out_h, layer_out))
    ]
    for copy in stores:
        copy.start()
    to_modes(grid_g, send_a.at[1], zweight(lanes, inv_zero, inv_rest))
    send(2, send_a.at[1])
    local[...] = dot(mix_b[...], whole(grid_g))
    receive(2, send_a.at[1])

    store_owned(owned(2), grad)
    for j in range(slab_half // GC):
        span = slice(j * half, (j + 1) * half)
        g_r = grad[0, :, span]
        g_i = grad[1, :, span]
        for c in range(chans):
            w_r = weight[0, c, :, span].astype(F32)
            w_i = weight[1, c, :, span].astype(F32)
            mode_grad[0, c : c + 1, span] = jnp.sum(w_r * g_r + w_i * g_i, axis=0, keepdims=True)
            mode_grad[1, c : c + 1, span] = jnp.sum(w_r * g_i - w_i * g_r, axis=0, keepdims=True)
    to_slabs(mode_grad, send_b.at[1], fwd_scale)
    send(3, send_b.at[1])
    for j in range(slab_half // GC):
        span = slice(j * half, (j + 1) * half)
        g_r = grad[0, :, span] * inv_wg
        g_i = grad[1, :, span] * inv_wg
        for c in range(chans):
            s_r = spec[0, c : c + 1, span]
            s_i = spec[1, c : c + 1, span]
            weight_grad[0, c, :, span] = g_r * s_r + g_i * s_i
            weight_grad[1, c, :, span] = g_i * s_r - g_r * s_i
    stores.append(pltpu.make_async_copy(weight_grad, weight_grad_h, store_sem.at[len(stores)]))
    stores[-1].start()
    receive(3, send_b.at[1])
    for h in range(halves):
        total = to_grid(3, h) + local[h * half_rows : (h + 1) * half_rows, :]
        field_grad[h * GC : (h + 1) * GC] = total.astype(BF).reshape(GC, rows_y, width)
    for d, s in by_x(field_grad_h, field_grad):
        stores.append(pltpu.make_async_copy(s, d, store_sem.at[len(stores)]))
        stores[-1].start()
    drain(0, send_a.at[0])
    drain(1, send_b.at[0])
    drain(2, send_a.at[1])
    drain(3, send_b.at[1])
    for copy in stores:
        copy.wait()


def on_device_fused(gx, gy, field, cotangent, spectral_weight, point_weight, bias):
    chans, rows_x, rows_y, nz_len = field.shape
    peers = gx * gy
    owned_modes = spectral_weight.shape[3]
    total_cells = gx * gy * rows_x * rows_y * nz_len
    mode_count = MX * MY * MZ
    inv = 1.0 / math.sqrt(2.0 * mode_count)
    zscales = (1.0 / math.sqrt(total_cells), inv, 2.0 * inv)
    wg_scale = math.sqrt(2.0 * mode_count / total_cells)
    tables = [jnp.asarray(t) for t in constant_tables(gx, gy, rows_x, rows_y, nz_len)]
    slab = MY // peers * chans
    lanes = 2 * MZ * rows_x
    rows, width = chans * rows_y, rows_x * nz_len
    vmem = pl.BlockSpec(memory_space=pltpu.VMEM)
    hbm = pl.BlockSpec(memory_space=pltpu.HBM)
    smem = pl.BlockSpec(memory_space=pltpu.SMEM)

    grid = pltpu.VMEM((chans, rows_y, width), BF)
    held = [t.shape[1:] if n < 2 else t.shape for n, t in enumerate(tables)]

    def body(*refs):
        fused(gx, gy, zscales, wg_scale, *refs)

    return pl.pallas_call(
        body,
        out_shape=(
            jax.ShapeDtypeStruct(field.shape, BF),
            jax.ShapeDtypeStruct(field.shape, BF),
            jax.ShapeDtypeStruct(spectral_weight.shape, F32),
        ),
        in_specs=[hbm, hbm, hbm, vmem, smem] + [hbm] * 6,
        out_specs=(hbm, hbm, hbm),
        scratch_shapes=[
            grid,
            grid,
            pltpu.VMEM(spectral_weight.shape, BF),
            *[pltpu.VMEM(s, BF) for s in held],
            grid,
            grid,
            pltpu.VMEM(spectral_weight.shape, F32),
            pltpu.VMEM((2, peers, slab, lanes), BF),
            pltpu.VMEM((2, gx, slab, lanes), BF),
            pltpu.VMEM((4, peers, slab, lanes), BF),
            grid,
            pltpu.VMEM((rows, width), F32),
            pltpu.VMEM((2, chans, owned_modes), F32),
            pltpu.VMEM((2, chans, owned_modes), F32),
            pltpu.VMEM((2, chans, owned_modes), F32),
            pltpu.VMEM((rows, rows), BF),
            pltpu.VMEM((rows, rows), BF),
            pltpu.SemaphoreType.DMA((4, peers)),
            pltpu.SemaphoreType.DMA((4, peers)),
            pltpu.SemaphoreType.DMA((2 * rows_x + 7,)),
            pltpu.SemaphoreType.DMA((2 * rows_x + 1,)),
        ],
        compiler_params=pltpu.CompilerParams(
            collective_id=0, has_side_effects=True, vmem_limit_bytes=56 * 1024 * 1024
        ),
    )(field, cotangent, spectral_weight, point_weight, bias, *tables)


def solution(mesh):
    gx, gy = mesh.shape["gx"], mesh.shape["gy"]
    in_specs = (
        P(None, ("groups", "gx"), "gy", None),
        P(None, ("groups", "gx"), "gy", None),
        P(None, None, None, ("gx", "gy")),
        P(),
        P(),
    )
    out_specs = (
        P(None, ("groups", "gx"), "gy", None),
        P(None, ("groups", "gx"), "gy", None),
        P("groups", None, None, ("gx", "gy")),
    )

    def local_program(field, cotangent, spectral_weight, point_weight, bias):
        rows_x = field.shape[1]
        fits = MY % (gx * gy) == 0 and MY // (gx * gy) * GC % 16 == 0
        fits = fits and 2 * MZ * rows_x == 128 and field.shape[0] % GC == 0
        if fits:
            return on_device_fused(gx, gy, field, cotangent, spectral_weight, point_weight, bias)
        return on_device(field, cotangent, spectral_weight, point_weight, bias)

    return jax.shard_map(
        local_program, mesh=mesh, in_specs=in_specs, out_specs=out_specs, check_vma=False
    )
```

```python
import functools
import math

import jax
import jax.numpy as jnp
import numpy as np
from jax import lax
from jax.experimental import pallas as pl
from jax.experimental.pallas import tpu as pltpu
from jax.sharding import PartitionSpec as P

MX = 32
MY = 32
MZ = 16


def phase_tables(count, length, offset, rows, signed):
    position = offset + jnp.arange(rows, dtype=jnp.int32)
    freq = jnp.arange(count, dtype=jnp.int32)
    if signed:
        freq = jnp.where(freq >= count // 2, freq + (length - count), freq)
    turns = freq[:, None] * position[None, :] % length
    angle = turns.astype(jnp.float32) * (2.0 * math.pi / length)
    return (jnp.cos(angle).astype(jnp.bfloat16), jnp.sin(angle).astype(jnp.bfloat16))


def z_transform(block, cos_z, sin_z):
    chans, rows_x, rows_y, nz_len = block.shape
    kept = cos_z.shape[0]
    tables = jnp.concatenate([cos_z, sin_z], axis=0)
    flat = jnp.dot(block.reshape(-1, nz_len), tables.T, preferred_element_type=jnp.float32)
    flat = flat.reshape(chans, rows_x, rows_y, 2 * kept)
    both = jnp.transpose(flat, (0, 3, 1, 2))
    return (both[:, :kept], both[:, kept:])


def point_mix(matrix, grid):
    chans = grid.shape[0]
    flat = jnp.dot(matrix, grid.reshape(chans, -1), preferred_element_type=jnp.float32)
    return flat.reshape(grid.shape)


def forward_yz(block, y_start, zscale, ny_total):
    hp = lax.Precision.HIGHEST
    rows_y = block.shape[2]
    nz_len = block.shape[3]
    cos_z, sin_z = phase_tables(MZ, nz_len, 0, nz_len, False)
    zscale_b = zscale[None, :, None, None]
    z_cos, z_sin = z_transform(block, cos_z, sin_z)
    part_r = z_cos * zscale_b
    part_i = -z_sin * zscale_b
    cos_y, sin_y = phase_tables(MY, ny_total, y_start, rows_y, True)
    cos_y = cos_y.astype(jnp.float32)
    sin_y = sin_y.astype(jnp.float32)
    out_r = jnp.einsum("ckxy,jy->cjkx", part_r, cos_y, precision=hp) + jnp.einsum(
        "ckxy,jy->cjkx", part_i, sin_y, precision=hp
    )
    out_i = jnp.einsum("ckxy,jy->cjkx", part_i, cos_y, precision=hp) - jnp.einsum(
        "ckxy,jy->cjkx", part_r, sin_y, precision=hp
    )
    return (out_r, out_i)


def forward_x(part_r, part_i, x_start, nx_total):
    hp = lax.Precision.HIGHEST
    chans = part_r.shape[0]
    rows_x = part_r.shape[3]
    cos_x, sin_x = phase_tables(MX, nx_total, x_start, rows_x, True)
    cos_x = cos_x.astype(jnp.float32)
    sin_x = sin_x.astype(jnp.float32)
    out_r = jnp.einsum("cjkx,ix->cjki", part_r, cos_x, precision=hp) + jnp.einsum(
        "cjkx,ix->cjki", part_i, sin_x, precision=hp
    )
    out_i = jnp.einsum("cjkx,ix->cjki", part_i, cos_x, precision=hp) - jnp.einsum(
        "cjkx,ix->cjki", part_r, sin_x, precision=hp
    )
    return jnp.stack([out_r.reshape(chans, -1), out_i.reshape(chans, -1)])


def inverse_modes(modes, x_start, y_start, zweight, nx_total, ny_total, rows_x, rows_y, nz_len):
    hp = lax.Precision.HIGHEST
    chans = modes.shape[1]
    values = modes.astype(jnp.float32).reshape(2, chans, MY, MZ, MX)
    mode_r = values[0]
    mode_i = values[1]
    cos_x, sin_x = phase_tables(MX, nx_total, x_start, rows_x, True)
    cos_x = cos_x.astype(jnp.float32)
    sin_x = sin_x.astype(jnp.float32)
    step_r = jnp.einsum("cjki,ix->cxjk", mode_r, cos_x, precision=hp) - jnp.einsum(
        "cjki,ix->cxjk", mode_i, sin_x, precision=hp
    )
    step_i = jnp.einsum("cjki,ix->cxjk", mode_i, cos_x, precision=hp) + jnp.einsum(
        "cjki,ix->cxjk", mode_r, sin_x, precision=hp
    )
    cos_y, sin_y = phase_tables(MY, ny_total, y_start, rows_y, True)
    cos_y = cos_y.astype(jnp.float32)
    sin_y = sin_y.astype(jnp.float32)
    next_r = jnp.einsum("cxjk,jy->cxyk", step_r, cos_y, precision=hp) - jnp.einsum(
        "cxjk,jy->cxyk", step_i, sin_y, precision=hp
    )
    next_i = jnp.einsum("cxjk,jy->cxyk", step_i, cos_y, precision=hp) + jnp.einsum(
        "cxjk,jy->cxyk", step_r, sin_y, precision=hp
    )
    cos_z, sin_z = phase_tables(MZ, nz_len, 0, nz_len, False)
    cos_z = cos_z.astype(jnp.float32)
    sin_z = sin_z.astype(jnp.float32)
    next_r = next_r * zweight
    next_i = next_i * zweight
    return jnp.einsum("cxyk,kz->cxyz", next_r, cos_z, precision=hp) - jnp.einsum(
        "cxyk,kz->cxyz", next_i, sin_z, precision=hp
    )


def channel_mix(spectrum, weight):
    hp = lax.Precision.HIGHEST
    w_r = weight[0].astype(jnp.float32)
    w_i = weight[1].astype(jnp.float32)
    out_r = jnp.einsum("im,iom->om", spectrum[0], w_r, precision=hp) - jnp.einsum(
        "im,iom->om", spectrum[1], w_i, precision=hp
    )
    out_i = jnp.einsum("im,iom->om", spectrum[1], w_r, precision=hp) + jnp.einsum(
        "im,iom->om", spectrum[0], w_i, precision=hp
    )
    return jnp.stack([out_r, out_i])


def mix_grads(spectrum, mixed_grad, weight):
    hp = lax.Precision.HIGHEST
    w_r = weight[0].astype(jnp.float32)
    w_i = weight[1].astype(jnp.float32)
    grad_r = jnp.einsum("om,im->iom", mixed_grad[0], spectrum[0], precision=hp) + jnp.einsum(
        "om,im->iom", mixed_grad[1], spectrum[1], precision=hp
    )
    grad_i = jnp.einsum("om,im->iom", mixed_grad[1], spectrum[0], precision=hp) - jnp.einsum(
        "om,im->iom", mixed_grad[0], spectrum[1], precision=hp
    )
    back_r = jnp.einsum("iom,om->im", w_r, mixed_grad[0], precision=hp) + jnp.einsum(
        "iom,om->im", w_i, mixed_grad[1], precision=hp
    )
    back_i = jnp.einsum("iom,om->im", w_r, mixed_grad[1], precision=hp) - jnp.einsum(
        "iom,om->im", w_i, mixed_grad[0], precision=hp
    )
    return (jnp.stack([grad_r, grad_i]), jnp.stack([back_r, back_i]))


def owned_spectrum(block, x_start, y_start, zscale, nx_total, ny_total):
    part_r, part_i = forward_yz(block, y_start, zscale, ny_total)
    whole = forward_x(part_r, part_i, x_start, nx_total)
    return lax.psum_scatter(whole, ("gx", "gy"), scatter_dimension=2, tiled=True)


def all_modes(owned_block):
    return lax.all_gather(owned_block, ("gx", "gy"), axis=2, tiled=True)


def on_device(field, cotangent, spectral_weight, point_weight, bias):
    rows_x = field.shape[1]
    rows_y = field.shape[2]
    nz_len = field.shape[3]
    nx_total = rows_x * lax.axis_size("gx")
    ny_total = rows_y * lax.axis_size("gy")
    total_cells = nx_total * ny_total * nz_len
    mode_count = MX * MY * MZ
    x_start = lax.axis_index("gx") * rows_x
    y_start = lax.axis_index("gy") * rows_y
    zindex = jnp.arange(MZ, dtype=jnp.int32)
    forward_scale = jnp.full((MZ,), 1.0 / math.sqrt(total_cells), jnp.float32)
    inverse_scale = jnp.where(zindex == 0, 1.0, 2.0).astype(jnp.float32) / math.sqrt(
        2.0 * mode_count
    )
    spectrum = owned_spectrum(field, x_start, y_start, forward_scale, nx_total, ny_total)
    mixed = channel_mix(spectrum, spectral_weight).astype(jnp.bfloat16)
    mixed_all = all_modes(mixed)
    spectral_out = inverse_modes(
        mixed_all, x_start, y_start, inverse_scale, nx_total, ny_total, rows_x, rows_y, nz_len
    )
    pre = spectral_out + point_mix(point_weight.T, field) + bias[:, None, None, None]
    layer_out = jax.nn.gelu(pre).astype(jnp.bfloat16)
    pre_grad = jax.vjp(jax.nn.gelu, pre)[1](cotangent.astype(jnp.float32))[0].astype(jnp.bfloat16)
    mixed_grad = owned_spectrum(pre_grad, x_start, y_start, inverse_scale, nx_total, ny_total)
    weight_grad, spectrum_grad = mix_grads(spectrum, mixed_grad, spectral_weight)
    weight_grad = weight_grad * math.sqrt(2.0 * mode_count / total_cells)
    grad_all = all_modes(spectrum_grad.astype(jnp.bfloat16))
    local = point_mix(point_weight, pre_grad)
    spectral = inverse_modes(
        grad_all, x_start, y_start, forward_scale, nx_total, ny_total, rows_x, rows_y, nz_len
    )
    field_grad = (local + spectral).astype(jnp.bfloat16)
    return (layer_out, field_grad, weight_grad)


BF = jnp.bfloat16
F32 = jnp.float32
MESH = pl.DeviceIdType.MESH
GC = 8


def host_tables(count, length, cells, signed):
    freq = np.arange(count)
    if signed:
        freq = np.where(freq >= count // 2, freq + (length - count), freq)
    turns = (freq[:, None] * cells[None, :]) % length
    angle = turns.astype(np.float32) * np.float32(2.0 * math.pi / length)
    rounded = [np.asarray(fn(angle)).astype(BF).astype(np.float32) for fn in (np.cos, np.sin)]
    return rounded[0], rounded[1]


def constant_tables(gx, gy, rows_x, rows_y, nz_len):
    nx_total, ny_total = rows_x * gx, rows_y * gy
    cos_x, sin_x = host_tables(MX, nx_total, np.arange(nx_total), True)
    cos_y, sin_y = host_tables(MY, ny_total, np.arange(ny_total), True)
    cos_z, sin_z = host_tables(MZ, nz_len, np.arange(nz_len), False)
    eye_c, eye_x, eye_k = np.eye(GC), np.eye(rows_x), np.eye(MZ)
    cy = cos_y.reshape(MY, gy, rows_y)
    sy = sin_y.reshape(MY, gy, rows_y)
    y_fwd = np.stack([np.einsum("jgy,cd->gjcdy", t, eye_c) for t in (cy, sy)], axis=1)
    y_fwd = y_fwd.reshape(gy, 2 * MY * GC, GC * rows_y)
    y_inv = np.stack([np.einsum("jgy,cd->gcyjd", t, eye_c) for t in (cy, -sy)], axis=3)
    y_inv = y_inv.reshape(gy, GC * rows_y, 2 * MY * GC)
    z_pairs = np.stack([np.stack([cos_z, -sin_z]), np.stack([-sin_z, -cos_z])])
    z_fwd = np.einsum("arkz,xw->axzrkw", z_pairs, eye_x)
    z_fwd = z_fwd.reshape(2 * rows_x * nz_len, 2 * MZ * rows_x)
    i_pairs = np.stack([np.stack([cos_z, -sin_z]), np.stack([sin_z, cos_z])])
    z_inv = np.einsum("arkz,xw->rkwaxz", i_pairs, eye_x)
    z_inv = z_inv.reshape(2 * MZ * rows_x, 2 * rows_x * nz_len)
    x_pairs = np.stack([np.stack([cos_x, -sin_x]), np.stack([sin_x, cos_x])])
    x_pairs = x_pairs.reshape(2, 2, MX, gx, rows_x)
    x_fwd = np.einsum("rsigx,kl->grkxsli", x_pairs, eye_k)
    x_fwd = x_fwd.reshape(gx * 2 * MZ * rows_x, 2 * MZ * MX)
    x_inv = np.ascontiguousarray(x_fwd.T)
    return [t.astype(BF) for t in (y_fwd, y_inv, z_fwd, z_inv, x_fwd, x_inv)]


def dot(a, b):
    return jnp.dot(a, b, preferred_element_type=F32)


def split_dot(a, b):
    high = a.astype(BF)
    low = (a - high.astype(F32)).astype(BF)
    both = dot(jnp.concatenate([high, low], axis=0), b)
    return both[: a.shape[0]] + both[a.shape[0] :]


def fused(
    gx, gy, zscales,
    field_h, cot_h, weight_h, point, bias, y_fwd_h, z_fwd_h, z_inv_h, y_inv_h, x_fwd_h, x_inv_h,
    layer_out_h, spec_h, grad_h, modes_h, local_h,
    field, cot, weight, y_fwd, z_fwd, z_inv, y_inv, x_fwd, x_inv, layer_out,
    send_a, send_b, recv, grid_g, local, spec, grad, mode_grad, mix_a, mix_b, send_sem, recv_sem,
    load_sem, store_sem,
):
    peers = gx * gy
    chans, rows_x, rows_y, nz_len = field_h.shape
    half_rows = GC * rows_y
    halves = chans // GC
    slab_half, lanes = recv.shape[3:]
    me_x, me_y = lax.axis_index("gx"), lax.axis_index("gy")
    me = me_x * gy + me_y
    half_modes = MZ * MX

    def peer(step):
        down = peers - 1 - step
        down = down - (down <= me).astype(jnp.int32)
        up = step + (step >= me).astype(jnp.int32)
        other = jnp.where(me < peers // 2, down, up)
        return other, {"gx": other // gy, "gy": lax.rem(other, gy)}

    barrier = pltpu.get_barrier_semaphore()
    loads = {}
    stores = []

    def store(source, target):
        stores.append(pltpu.make_async_copy(source, target, store_sem.at[len(stores)]))
        stores[-1].start()


    def load(name, *pairs):
        copies = []
        for source, target in pairs:
            count = sum(len(c) for c in loads.values()) + len(copies)
            copies.append(pltpu.make_async_copy(source, target, load_sem.at[count]))
            copies[-1].start()
        loads[name] = copies

    def loaded(*names):
        for name in names:
            for copy in loads[name]:
                copy.wait()

    def by_x(flat, grid):
        return [
            (flat.at[:, x], grid.at[:, :, x * nz_len : (x + 1) * nz_len]) for x in range(rows_x)
        ]

    load("field", *by_x(field_h, field))
    load("y_fwd", (y_fwd_h.at[me_y], y_fwd))
    load("z_fwd", (z_fwd_h, z_fwd))
    load("x_fwd", (x_fwd_h, x_fwd))
    load("weight", (weight_h, weight))
    load("x_inv", (x_inv_h, x_inv))
    load("z_inv", (z_inv_h, z_inv))
    load("y_inv", (y_inv_h.at[me_y], y_inv))
    load("cot", *by_x(cot_h, cot))

    def greet(step, carry):
        pl.semaphore_signal(barrier, inc=1, device_id=peer(step)[1], device_id_type=MESH)
        return carry

    lax.fori_loop(0, peers - 1, greet, 0, unroll=True)

    def copy_to(phase, h, step):
        other, where = peer(step)
        buffer = send_a.at[phase // 2, h, other] if phase % 2 == 0 else send_b.at[phase // 2, h, other // gy]
        return pltpu.make_async_remote_copy(
            src_ref=buffer,
            dst_ref=recv.at[phase, h, me],
            send_sem=send_sem.at[phase, h, other],
            recv_sem=recv_sem.at[phase, h, me],
            device_id=where,
            device_id_type=MESH,
        )

    def send(phase, h):
        def one(step, carry):
            copy_to(phase, h, step).start()
            return carry

        lax.fori_loop(0, peers - 1, one, 0, unroll=True)
        if phase % 2 == 0:
            recv[phase, h, me] = send_a[phase // 2, h, me]
        else:
            recv[phase, h, me] = send_b[phase // 2, h, me_x]

    def receive(phase, h):
        def one(step, carry):
            other, where = peer(step)
            pltpu.make_async_remote_copy(
                src_ref=recv.at[phase, h, other],
                dst_ref=recv.at[phase, h, other],
                send_sem=send_sem.at[phase, h, other],
                recv_sem=recv_sem.at[phase, h, other],
                device_id=where,
                device_id_type=MESH,
            ).wait_recv()
            return carry

        lax.fori_loop(0, peers - 1, one, 0, unroll=True)

    def drain(phase):
        def one(step, carry):
            for h in range(halves):
                copy_to(phase, h, step).wait_send()
            return carry

        lax.fori_loop(0, peers - 1, one, 0, unroll=True)

    def zweight(width, scale_zero, scale_rest):
        lane = lax.broadcasted_iota(jnp.int32, (1, width), 1)
        k = lax.rem(lane // rows_x, MZ)
        return jnp.where(k == 0, scale_zero, scale_rest).astype(F32)

    fwd_scale, inv_zero, inv_rest = zscales

    width = rows_x * nz_len

    def grid_half(grid, h):
        return grid[h * GC : (h + 1) * GC].reshape(half_rows, width)

    def whole(grid):
        return grid[...].reshape(chans * rows_y, width)

    def to_modes(grid, phase, h, scale):
        after_y = dot(y_fwd[...], grid_half(grid, h))
        rows = after_y.shape[0] // 2
        both = jnp.concatenate([after_y[:rows], after_y[rows:]], axis=1).astype(BF)
        out = (dot(both, z_fwd[...]) * scale).astype(BF)
        send_a[phase // 2, h] = out.reshape(peers, slab_half, lanes)

    def owned(phase, h, store):
        parts = []
        for s in range(gx):
            total = recv[phase, h, s * gy].astype(F32)
            for u in range(1, gy):
                total = total + recv[phase, h, s * gy + u].astype(F32)
            parts.append(total)
        values = split_dot(jnp.concatenate(parts, axis=1), x_fwd[...])
        for j in range(slab_half // GC):
            for r in range(2):
                store[r, h * GC : (h + 1) * GC, j * half_modes : (j + 1) * half_modes] = values[
                    j * GC : (j + 1) * GC, r * half_modes : (r + 1) * half_modes
                ]

    def to_slabs(store, phase, scale):
        rows = []
        for h in range(halves):
            for j in range(slab_half // GC):
                rows.append(
                    jnp.concatenate(
                        [
                            store[r, h * GC : (h + 1) * GC, j * half_modes : (j + 1) * half_modes]
                            for r in range(2)
                        ],
                        axis=1,
                    )
                )
        values = jnp.concatenate(rows, axis=0).astype(BF)
        out = (dot(values, x_inv[...]) * scale).astype(BF)
        for s in range(gx):
            for h in range(halves):
                send_b[phase // 2, h, s] = out[
                    h * slab_half : (h + 1) * slab_half, s * lanes : (s + 1) * lanes
                ]

    def spread(matrix):
        n = chans * rows_y
        row = lax.broadcasted_iota(jnp.int32, (n, chans), 0) // rows_y
        pick = (row == lax.broadcasted_iota(jnp.int32, (n, chans), 1)).astype(BF)
        col = lax.broadcasted_iota(jnp.int32, (chans, n), 1) // rows_y
        pick_t = (col == lax.broadcasted_iota(jnp.int32, (chans, n), 0)).astype(BF)
        wide = dot(dot(pick, matrix).astype(BF), pick_t)
        diag = lax.rem(lax.broadcasted_iota(jnp.int32, (n, n), 0), rows_y) == lax.rem(
            lax.broadcasted_iota(jnp.int32, (n, n), 1), rows_y
        )
        return jnp.where(diag, wide, 0.0).astype(BF)

    loaded("field", "y_fwd", "z_fwd")
    for h in range(halves):
        to_modes(field, 0, h, fwd_scale)
        if h == 0:
            pl.semaphore_wait(barrier, peers - 1)
        send(0, h)
    mix_a[...] = spread(point[...].T)
    mix_b[...] = spread(point[...])
    local[...] = dot(mix_a[...], whole(field))

    loaded("x_fwd", "weight", "x_inv")
    half = half_modes
    mixed = {}
    for h in range(halves):
        receive(0, h)
        owned(0, h, spec)
        for j in range(slab_half // GC):
            span = slice(j * half, (j + 1) * half)
            mixed_r, mixed_i = mixed.get(j, (0.0, 0.0))
            for c in range(h * GC, (h + 1) * GC):
                w_r = weight[0, c, :, span].astype(F32)
                w_i = weight[1, c, :, span].astype(F32)
                s_r = spec[0, c : c + 1, span]
                s_i = spec[1, c : c + 1, span]
                mixed_r = mixed_r + (s_r * w_r - s_i * w_i)
                mixed_i = mixed_i + (s_i * w_r + s_r * w_i)
            mixed[j] = (mixed_r, mixed_i)
    for j in range(slab_half // GC):
        span = slice(j * half, (j + 1) * half)
        grad[0, :, span] = mixed[j][0]
        grad[1, :, span] = mixed[j][1]
    to_slabs(grad, 1, zweight(gx * lanes, inv_zero, inv_rest))
    for h in range(halves):
        send(1, h)

    loaded("z_inv", "y_inv", "cot")
    a = math.sqrt(2.0 / math.pi)
    for h in range(halves):
        rows = slice(h * half_rows, (h + 1) * half_rows)
        receive(1, h)
        pre_half = to_grid(recv[1, h], z_inv[...], y_inv[...]) + local[rows, :]
        for c in range(GC):
            o = h * GC + c
            pre = pre_half[c * rows_y : (c + 1) * rows_y] + bias[o]
            square = pre * pre
            t = jnp.tanh(a * pre * (1.0 + 0.044715 * square))
            cdf = 0.5 * (1.0 + t)
            out = (pre * cdf).astype(BF)
            slope = cdf + 0.5 * pre * (1.0 - t * t) * (a * (1.0 + 3.0 * 0.044715 * square))
            layer_out[o] = out
            grid_g[o] = (cot[o].astype(F32) * slope).astype(BF)
        some = slice(h * GC, (h + 1) * GC)
        for target, source in by_x(layer_out_h.at[some], layer_out.at[some]):
            store(source, target)
        to_modes(grid_g, 2, h, zweight(lanes, inv_zero, inv_rest))
        send(2, h)
    local[...] = dot(mix_b[...], whole(grid_g))
    store(local, local_h)

    for h in range(halves):
        receive(2, h)
        owned(2, h, grad)
    for j in range(slab_half // GC):
        span = slice(j * half, (j + 1) * half)
        g_r = grad[0, :, span]
        g_i = grad[1, :, span]
        for c in range(chans):
            w_r = weight[0, c, :, span].astype(F32)
            w_i = weight[1, c, :, span].astype(F32)
            mode_grad[0, c : c + 1, span] = jnp.sum(w_r * g_r + w_i * g_i, axis=0, keepdims=True)
            mode_grad[1, c : c + 1, span] = jnp.sum(w_r * g_i - w_i * g_r, axis=0, keepdims=True)
    to_slabs(mode_grad, 3, fwd_scale)
    for h in range(halves):
        send(3, h)
    store(spec, spec_h)
    store(grad, grad_h)
    for h in range(halves):
        receive(3, h)
        store(recv.at[3, h], modes_h.at[h])
    for phase in range(4):
        drain(phase)
    for copy in stores:
        copy.wait()


def to_grid(modes, z_table, y_table):
    peers, slab_half, lanes = modes.shape
    after_z = dot(modes.reshape(peers * slab_half, lanes), z_table).astype(BF)
    width = after_z.shape[1] // 2
    both = jnp.concatenate([after_z[:, :width], after_z[:, width:]], axis=0)
    return dot(y_table, both)


def results(
    wg_scale, first_h, spec_h, grad_h, modes_h, local_h, z_inv_h, y_inv_h,
    layer_out_h, field_grad_h, weight_grad_h,
    first, spec, grad, modes, local, z_inv, y_inv, field_grad, weight_grad, sem,
):
    chans, rows_x, rows_y, nz_len = layer_out_h.shape
    half_rows = GC * rows_y

    def copy(source, target):
        copies.append(pltpu.make_async_copy(source, target, sem.at[len(copies)]))
        copies[-1].start()

    copies = []
    copy(spec_h, spec)
    copy(grad_h, grad)
    copy(modes_h, modes)
    copy(z_inv_h, z_inv)
    copy(y_inv_h.at[lax.axis_index("gy")], y_inv)
    copy(first_h, first)
    copy(local_h, local)
    copies[0].wait()
    copies[1].wait()
    quarter = chans // 4
    for q in range(4):
        some = slice(q * quarter, (q + 1) * quarter)
        for c in range(q * quarter, (q + 1) * quarter):
            s_r, s_i = spec[0, c : c + 1, :] * wg_scale, spec[1, c : c + 1, :] * wg_scale
            weight_grad[0, c] = grad[0] * s_r + grad[1] * s_i
            weight_grad[1, c] = grad[1] * s_r - grad[0] * s_i
        copy(weight_grad.at[:, some], weight_grad_h.at[:, some])
    copies[5].wait()
    copy(first, layer_out_h)
    for n in (2, 3, 4, 6):
        copies[n].wait()
    for h in range(modes.shape[0]):
        some = slice(h * GC, (h + 1) * GC)
        total = to_grid(modes[h], z_inv[...], y_inv[...]) + local[h * half_rows : (h + 1) * half_rows, :]
        field_grad[some] = total.astype(BF).reshape(GC, rows_y, rows_x * nz_len)
        for x in range(rows_x):
            copy(field_grad.at[some, :, x * nz_len : (x + 1) * nz_len], field_grad_h.at[some, x])
    for started in copies[7:]:
        started.wait()


def on_device_fused(gx, gy, field, cotangent, spectral_weight, point_weight, bias):
    chans, rows_x, rows_y, nz_len = field.shape
    peers = gx * gy
    owned_modes = spectral_weight.shape[3]
    total_cells = gx * gy * rows_x * rows_y * nz_len
    mode_count = MX * MY * MZ
    inv = 1.0 / math.sqrt(2.0 * mode_count)
    zscales = (1.0 / math.sqrt(total_cells), inv, 2.0 * inv)
    wg_scale = math.sqrt(2.0 * mode_count / total_cells)
    tables = [jnp.asarray(t) for t in constant_tables(gx, gy, rows_x, rows_y, nz_len)]
    y_fwd, y_inv, z_fwd, z_inv, x_fwd, x_inv = tables
    halves = chans // GC
    slab_half = MY // peers * GC
    lanes = 2 * MZ * rows_x
    rows, width = chans * rows_y, rows_x * nz_len
    vmem = pl.BlockSpec(memory_space=pltpu.VMEM)
    smem = pl.BlockSpec(memory_space=pltpu.SMEM)
    hbm = pl.BlockSpec(memory_space=pltpu.HBM)
    grid = pltpu.VMEM((chans, rows_y, width), BF)
    modes = pltpu.VMEM((2, chans, owned_modes), F32)

    def body(*refs):
        fused(gx, gy, zscales, *refs)

    layer_out, spec, grad, grad_modes, local = pl.pallas_call(
        body,
        out_shape=(
            jax.ShapeDtypeStruct(field.shape, BF),
            jax.ShapeDtypeStruct(modes.shape, F32),
            jax.ShapeDtypeStruct(modes.shape, F32),
            jax.ShapeDtypeStruct((halves, peers, slab_half, lanes), BF),
            jax.ShapeDtypeStruct((rows, width), F32),
        ),
        in_specs=[hbm, hbm, hbm, vmem, smem] + [hbm] * 6,
        out_specs=(hbm,) * 5,
        scratch_shapes=[
            grid,
            grid,
            pltpu.VMEM(spectral_weight.shape, BF),
            pltpu.VMEM(y_fwd.shape[1:], BF),
            pltpu.VMEM(z_fwd.shape, BF),
            pltpu.VMEM(z_inv.shape, BF),
            pltpu.VMEM(y_inv.shape[1:], BF),
            pltpu.VMEM(x_fwd.shape, BF),
            pltpu.VMEM(x_inv.shape, BF),
            grid,
            pltpu.VMEM((2, halves, peers, slab_half, lanes), BF),
            pltpu.VMEM((2, halves, gx, slab_half, lanes), BF),
            pltpu.VMEM((4, halves, peers, slab_half, lanes), BF),
            grid,
            pltpu.VMEM((rows, width), F32),
            modes,
            modes,
            modes,
            pltpu.VMEM((rows, rows), BF),
            pltpu.VMEM((rows, rows), BF),
            pltpu.SemaphoreType.DMA((4, halves, peers)),
            pltpu.SemaphoreType.DMA((4, halves, peers)),
            pltpu.SemaphoreType.DMA((2 * rows_x + 7,)),
            pltpu.SemaphoreType.DMA((halves * (rows_x + 1) + 3,)),
        ],
        compiler_params=pltpu.CompilerParams(
            collective_id=0, has_side_effects=True, vmem_limit_bytes=56 * 1024 * 1024
        ),
    )(field, cotangent, spectral_weight, point_weight, bias, y_fwd, z_fwd, z_inv, y_inv, x_fwd, x_inv)
    return pl.pallas_call(
        functools.partial(results, wg_scale),
        out_shape=(
            jax.ShapeDtypeStruct(field.shape, BF),
            jax.ShapeDtypeStruct(field.shape, BF),
            jax.ShapeDtypeStruct(spectral_weight.shape, F32),
        ),
        in_specs=[hbm] * 7,
        out_specs=(hbm, hbm, hbm),
        scratch_shapes=[
            pltpu.VMEM(field.shape, BF),
            modes,
            modes,
            pltpu.VMEM(grad_modes.shape, BF),
            pltpu.VMEM(local.shape, F32),
            pltpu.VMEM(z_inv.shape, BF),
            pltpu.VMEM(y_inv.shape[1:], BF),
            grid,
            pltpu.VMEM(spectral_weight.shape, F32),
            pltpu.SemaphoreType.DMA((12 + halves * rows_x,)),
        ],
        compiler_params=pltpu.CompilerParams(vmem_limit_bytes=56 * 1024 * 1024),
    )(layer_out, spec, grad, grad_modes, local, z_inv, y_inv)


def solution(mesh):
    gx, gy = mesh.shape["gx"], mesh.shape["gy"]
    in_specs = (
        P(None, ("groups", "gx"), "gy", None),
        P(None, ("groups", "gx"), "gy", None),
        P(None, None, None, ("gx", "gy")),
        P(),
        P(),
    )
    out_specs = (
        P(None, ("groups", "gx"), "gy", None),
        P(None, ("groups", "gx"), "gy", None),
        P("groups", None, None, ("gx", "gy")),
    )

    def local_program(field, cotangent, spectral_weight, point_weight, bias):
        rows_x = field.shape[1]
        fits = MY % (gx * gy) == 0 and MY // (gx * gy) * GC % 16 == 0
        fits = fits and 2 * MZ * rows_x == 128 and field.shape[0] % GC == 0
        if fits:
            return on_device_fused(gx, gy, field, cotangent, spectral_weight, point_weight, bias)
        return on_device(field, cotangent, spectral_weight, point_weight, bias)

    return jax.shard_map(
        local_program, mesh=mesh, in_specs=in_specs, out_specs=out_specs, check_vma=False
    )
```

```python
import functools
import math

import jax
import jax.numpy as jnp
import numpy as np
from jax import lax
from jax.experimental import pallas as pl
from jax.experimental.pallas import tpu as pltpu
from jax.sharding import PartitionSpec as P

MX = 32
MY = 32
MZ = 16


def phase_tables(count, length, offset, rows, signed):
    position = offset + jnp.arange(rows, dtype=jnp.int32)
    freq = jnp.arange(count, dtype=jnp.int32)
    if signed:
        freq = jnp.where(freq >= count // 2, freq + (length - count), freq)
    turns = freq[:, None] * position[None, :] % length
    angle = turns.astype(jnp.float32) * (2.0 * math.pi / length)
    return (jnp.cos(angle).astype(jnp.bfloat16), jnp.sin(angle).astype(jnp.bfloat16))


def z_transform(block, cos_z, sin_z):
    chans, rows_x, rows_y, nz_len = block.shape
    kept = cos_z.shape[0]
    tables = jnp.concatenate([cos_z, sin_z], axis=0)
    flat = jnp.dot(block.reshape(-1, nz_len), tables.T, preferred_element_type=jnp.float32)
    flat = flat.reshape(chans, rows_x, rows_y, 2 * kept)
    both = jnp.transpose(flat, (0, 3, 1, 2))
    return (both[:, :kept], both[:, kept:])


def point_mix(matrix, grid):
    chans = grid.shape[0]
    flat = jnp.dot(matrix, grid.reshape(chans, -1), preferred_element_type=jnp.float32)
    return flat.reshape(grid.shape)


def forward_yz(block, y_start, zscale, ny_total):
    hp = lax.Precision.HIGHEST
    rows_y = block.shape[2]
    nz_len = block.shape[3]
    cos_z, sin_z = phase_tables(MZ, nz_len, 0, nz_len, False)
    zscale_b = zscale[None, :, None, None]
    z_cos, z_sin = z_transform(block, cos_z, sin_z)
    part_r = z_cos * zscale_b
    part_i = -z_sin * zscale_b
    cos_y, sin_y = phase_tables(MY, ny_total, y_start, rows_y, True)
    cos_y = cos_y.astype(jnp.float32)
    sin_y = sin_y.astype(jnp.float32)
    out_r = jnp.einsum("ckxy,jy->cjkx", part_r, cos_y, precision=hp) + jnp.einsum(
        "ckxy,jy->cjkx", part_i, sin_y, precision=hp
    )
    out_i = jnp.einsum("ckxy,jy->cjkx", part_i, cos_y, precision=hp) - jnp.einsum(
        "ckxy,jy->cjkx", part_r, sin_y, precision=hp
    )
    return (out_r, out_i)


def forward_x(part_r, part_i, x_start, nx_total):
    hp = lax.Precision.HIGHEST
    chans = part_r.shape[0]
    rows_x = part_r.shape[3]
    cos_x, sin_x = phase_tables(MX, nx_total, x_start, rows_x, True)
    cos_x = cos_x.astype(jnp.float32)
    sin_x = sin_x.astype(jnp.float32)
    out_r = jnp.einsum("cjkx,ix->cjki", part_r, cos_x, precision=hp) + jnp.einsum(
        "cjkx,ix->cjki", part_i, sin_x, precision=hp
    )
    out_i = jnp.einsum("cjkx,ix->cjki", part_i, cos_x, precision=hp) - jnp.einsum(
        "cjkx,ix->cjki", part_r, sin_x, precision=hp
    )
    return jnp.stack([out_r.reshape(chans, -1), out_i.reshape(chans, -1)])


def inverse_modes(modes, x_start, y_start, zweight, nx_total, ny_total, rows_x, rows_y, nz_len):
    hp = lax.Precision.HIGHEST
    chans = modes.shape[1]
    values = modes.astype(jnp.float32).reshape(2, chans, MY, MZ, MX)
    mode_r = values[0]
    mode_i = values[1]
    cos_x, sin_x = phase_tables(MX, nx_total, x_start, rows_x, True)
    cos_x = cos_x.astype(jnp.float32)
    sin_x = sin_x.astype(jnp.float32)
    step_r = jnp.einsum("cjki,ix->cxjk", mode_r, cos_x, precision=hp) - jnp.einsum(
        "cjki,ix->cxjk", mode_i, sin_x, precision=hp
    )
    step_i = jnp.einsum("cjki,ix->cxjk", mode_i, cos_x, precision=hp) + jnp.einsum(
        "cjki,ix->cxjk", mode_r, sin_x, precision=hp
    )
    cos_y, sin_y = phase_tables(MY, ny_total, y_start, rows_y, True)
    cos_y = cos_y.astype(jnp.float32)
    sin_y = sin_y.astype(jnp.float32)
    next_r = jnp.einsum("cxjk,jy->cxyk", step_r, cos_y, precision=hp) - jnp.einsum(
        "cxjk,jy->cxyk", step_i, sin_y, precision=hp
    )
    next_i = jnp.einsum("cxjk,jy->cxyk", step_i, cos_y, precision=hp) + jnp.einsum(
        "cxjk,jy->cxyk", step_r, sin_y, precision=hp
    )
    cos_z, sin_z = phase_tables(MZ, nz_len, 0, nz_len, False)
    cos_z = cos_z.astype(jnp.float32)
    sin_z = sin_z.astype(jnp.float32)
    next_r = next_r * zweight
    next_i = next_i * zweight
    return jnp.einsum("cxyk,kz->cxyz", next_r, cos_z, precision=hp) - jnp.einsum(
        "cxyk,kz->cxyz", next_i, sin_z, precision=hp
    )


def channel_mix(spectrum, weight):
    hp = lax.Precision.HIGHEST
    w_r = weight[0].astype(jnp.float32)
    w_i = weight[1].astype(jnp.float32)
    out_r = jnp.einsum("im,iom->om", spectrum[0], w_r, precision=hp) - jnp.einsum(
        "im,iom->om", spectrum[1], w_i, precision=hp
    )
    out_i = jnp.einsum("im,iom->om", spectrum[1], w_r, precision=hp) + jnp.einsum(
        "im,iom->om", spectrum[0], w_i, precision=hp
    )
    return jnp.stack([out_r, out_i])


def mix_grads(spectrum, mixed_grad, weight):
    hp = lax.Precision.HIGHEST
    w_r = weight[0].astype(jnp.float32)
    w_i = weight[1].astype(jnp.float32)
    grad_r = jnp.einsum("om,im->iom", mixed_grad[0], spectrum[0], precision=hp) + jnp.einsum(
        "om,im->iom", mixed_grad[1], spectrum[1], precision=hp
    )
    grad_i = jnp.einsum("om,im->iom", mixed_grad[1], spectrum[0], precision=hp) - jnp.einsum(
        "om,im->iom", mixed_grad[0], spectrum[1], precision=hp
    )
    back_r = jnp.einsum("iom,om->im", w_r, mixed_grad[0], precision=hp) + jnp.einsum(
        "iom,om->im", w_i, mixed_grad[1], precision=hp
    )
    back_i = jnp.einsum("iom,om->im", w_r, mixed_grad[1], precision=hp) - jnp.einsum(
        "iom,om->im", w_i, mixed_grad[0], precision=hp
    )
    return (jnp.stack([grad_r, grad_i]), jnp.stack([back_r, back_i]))


def owned_spectrum(block, x_start, y_start, zscale, nx_total, ny_total):
    part_r, part_i = forward_yz(block, y_start, zscale, ny_total)
    whole = forward_x(part_r, part_i, x_start, nx_total)
    return lax.psum_scatter(whole, ("gx", "gy"), scatter_dimension=2, tiled=True)


def all_modes(owned_block):
    return lax.all_gather(owned_block, ("gx", "gy"), axis=2, tiled=True)


def on_device(field, cotangent, spectral_weight, point_weight, bias):
    rows_x = field.shape[1]
    rows_y = field.shape[2]
    nz_len = field.shape[3]
    nx_total = rows_x * lax.axis_size("gx")
    ny_total = rows_y * lax.axis_size("gy")
    total_cells = nx_total * ny_total * nz_len
    mode_count = MX * MY * MZ
    x_start = lax.axis_index("gx") * rows_x
    y_start = lax.axis_index("gy") * rows_y
    zindex = jnp.arange(MZ, dtype=jnp.int32)
    forward_scale = jnp.full((MZ,), 1.0 / math.sqrt(total_cells), jnp.float32)
    inverse_scale = jnp.where(zindex == 0, 1.0, 2.0).astype(jnp.float32) / math.sqrt(
        2.0 * mode_count
    )
    spectrum = owned_spectrum(field, x_start, y_start, forward_scale, nx_total, ny_total)
    mixed = channel_mix(spectrum, spectral_weight).astype(jnp.bfloat16)
    mixed_all = all_modes(mixed)
    spectral_out = inverse_modes(
        mixed_all, x_start, y_start, inverse_scale, nx_total, ny_total, rows_x, rows_y, nz_len
    )
    pre = spectral_out + point_mix(point_weight.T, field) + bias[:, None, None, None]
    layer_out = jax.nn.gelu(pre).astype(jnp.bfloat16)
    pre_grad = jax.vjp(jax.nn.gelu, pre)[1](cotangent.astype(jnp.float32))[0].astype(jnp.bfloat16)
    mixed_grad = owned_spectrum(pre_grad, x_start, y_start, inverse_scale, nx_total, ny_total)
    weight_grad, spectrum_grad = mix_grads(spectrum, mixed_grad, spectral_weight)
    weight_grad = weight_grad * math.sqrt(2.0 * mode_count / total_cells)
    grad_all = all_modes(spectrum_grad.astype(jnp.bfloat16))
    local = point_mix(point_weight, pre_grad)
    spectral = inverse_modes(
        grad_all, x_start, y_start, forward_scale, nx_total, ny_total, rows_x, rows_y, nz_len
    )
    field_grad = (local + spectral).astype(jnp.bfloat16)
    return (layer_out, field_grad, weight_grad)


BF = jnp.bfloat16
F32 = jnp.float32
MESH = pl.DeviceIdType.MESH
GC = 8


def host_tables(count, length, cells, signed):
    freq = np.arange(count)
    if signed:
        freq = np.where(freq >= count // 2, freq + (length - count), freq)
    turns = (freq[:, None] * cells[None, :]) % length
    angle = turns.astype(np.float32) * np.float32(2.0 * math.pi / length)
    rounded = [np.asarray(fn(angle)).astype(BF).astype(np.float32) for fn in (np.cos, np.sin)]
    return rounded[0], rounded[1]


def constant_tables(gx, gy, rows_x, rows_y, nz_len):
    nx_total, ny_total = rows_x * gx, rows_y * gy
    cos_x, sin_x = host_tables(MX, nx_total, np.arange(nx_total), True)
    cos_y, sin_y = host_tables(MY, ny_total, np.arange(ny_total), True)
    cos_z, sin_z = host_tables(MZ, nz_len, np.arange(nz_len), False)
    eye_c, eye_x, eye_k = np.eye(GC), np.eye(rows_x), np.eye(MZ)
    cy = cos_y.reshape(MY, gy, rows_y)
    sy = sin_y.reshape(MY, gy, rows_y)
    y_fwd = np.stack([np.einsum("jgy,cd->gjcdy", t, eye_c) for t in (cy, sy)], axis=1)
    y_fwd = y_fwd.reshape(gy, 2 * MY * GC, GC * rows_y)
    y_inv = np.stack([np.einsum("jgy,cd->gcyjd", t, eye_c) for t in (cy, -sy)], axis=3)
    y_inv = y_inv.reshape(gy, GC * rows_y, 2 * MY * GC)
    z_pairs = np.stack([np.stack([cos_z, -sin_z]), np.stack([-sin_z, -cos_z])])
    z_fwd = np.einsum("arkz,xw->axzrkw", z_pairs, eye_x)
    z_fwd = z_fwd.reshape(2 * rows_x * nz_len, 2 * MZ * rows_x)
    i_pairs = np.stack([np.stack([cos_z, -sin_z]), np.stack([sin_z, cos_z])])
    z_inv = np.einsum("arkz,xw->rkwaxz", i_pairs, eye_x)
    z_inv = z_inv.reshape(2 * MZ * rows_x, 2 * rows_x * nz_len)
    x_pairs = np.stack([np.stack([cos_x, -sin_x]), np.stack([sin_x, cos_x])])
    x_pairs = x_pairs.reshape(2, 2, MX, gx, rows_x)
    x_fwd = np.einsum("rsigx,kl->grkxsli", x_pairs, eye_k)
    x_fwd = x_fwd.reshape(gx * 2 * MZ * rows_x, 2 * MZ * MX)
    x_inv = np.ascontiguousarray(x_fwd.T)
    return [t.astype(BF) for t in (y_fwd, y_inv, z_fwd, z_inv, x_fwd, x_inv)]


def dot(a, b):
    return jnp.dot(a, b, preferred_element_type=F32)


def split_dot(a, b):
    high = a.astype(BF)
    low = (a - high.astype(F32)).astype(BF)
    both = dot(jnp.concatenate([high, low], axis=0), b)
    return both[: a.shape[0]] + both[a.shape[0] :]


def fused(
    gx, gy, zscales,
    field_h, cot_h, weight_h, point_h, bias_h, y_fwd_h, z_fwd_h, z_inv_h, y_inv_h, x_fwd_h, x_inv_h,
    layer_out_h, spec_h, grad_h, modes_h, local_h,
    field, cot, weight, point, bias, y_fwd, z_fwd, z_inv, y_inv, x_fwd, x_inv, layer_out,
    send_a, send_b, recv, grid_g, local, spec, grad, mode_grad, mix_a, mix_b, send_sem, recv_sem,
    load_sem, store_sem,
):
    peers = gx * gy
    chans, rows_x, rows_y, nz_len = field_h.shape
    half_rows = GC * rows_y
    halves = chans // GC
    slab_half, lanes = recv.shape[3:]
    me_x, me_y = lax.axis_index("gx"), lax.axis_index("gy")
    me = me_x * gy + me_y
    half_modes = MZ * MX

    def peer(step):
        down = peers - 1 - step
        down = down - (down <= me).astype(jnp.int32)
        up = step + (step >= me).astype(jnp.int32)
        other = jnp.where(me < peers // 2, down, up)
        return other, {"gx": other // gy, "gy": lax.rem(other, gy)}

    barrier = pltpu.get_barrier_semaphore()
    loads = {}
    stores = []

    def store(source, target):
        stores.append(pltpu.make_async_copy(source, target, store_sem.at[len(stores)]))
        stores[-1].start()


    def load(name, *pairs):
        copies = []
        for source, target in pairs:
            count = sum(len(c) for c in loads.values()) + len(copies)
            copies.append(pltpu.make_async_copy(source, target, load_sem.at[count]))
            copies[-1].start()
        loads[name] = copies

    def loaded(*names):
        for name in names:
            for copy in loads[name]:
                copy.wait()

    def by_x(flat, grid):
        return [
            (flat.at[:, x], grid.at[:, :, x * nz_len : (x + 1) * nz_len]) for x in range(rows_x)
        ]

    load("field", *by_x(field_h, field))
    load("y_fwd", (y_fwd_h.at[me_y], y_fwd))
    load("z_fwd", (z_fwd_h, z_fwd))
    load("point", (point_h, point))
    load("bias", (bias_h, bias))
    load("x_fwd", (x_fwd_h, x_fwd))
    load("weight", (weight_h, weight))
    load("x_inv", (x_inv_h, x_inv))
    load("z_inv", (z_inv_h, z_inv))
    load("y_inv", (y_inv_h.at[me_y], y_inv))
    load("cot", *by_x(cot_h, cot))

    def greet(step, carry):
        pl.semaphore_signal(barrier, inc=1, device_id=peer(step)[1], device_id_type=MESH)
        return carry

    lax.fori_loop(0, peers - 1, greet, 0, unroll=True)

    def copy_to(phase, h, step):
        other, where = peer(step)
        buffer = send_a.at[phase // 2, h, other] if phase % 2 == 0 else send_b.at[phase // 2, h, other // gy]
        return pltpu.make_async_remote_copy(
            src_ref=buffer,
            dst_ref=recv.at[phase, h, me],
            send_sem=send_sem.at[phase, h],
            recv_sem=recv_sem.at[phase, h],
            device_id=where,
            device_id_type=MESH,
        )

    def send(phase, h):
        def one(step, carry):
            copy_to(phase, h, step).start()
            return carry

        lax.fori_loop(0, peers - 1, one, 0, unroll=True)
        if phase % 2 == 0:
            recv[phase, h, me] = send_a[phase // 2, h, me]
        else:
            recv[phase, h, me] = send_b[phase // 2, h, me_x]

    def all_slabs(phase, h):
        slabs = recv.at[phase, h, pl.ds(0, peers - 1)]
        return pltpu.make_async_remote_copy(
            src_ref=slabs,
            dst_ref=slabs,
            send_sem=send_sem.at[phase, h],
            recv_sem=recv_sem.at[phase, h],
            device_id=peer(0)[1],
            device_id_type=MESH,
        )

    def receive(phase, h):
        all_slabs(phase, h).wait_recv()

    def drain(phase):
        for h in range(halves):
            all_slabs(phase, h).wait_send()

    def zweight(width, scale_zero, scale_rest):
        lane = lax.broadcasted_iota(jnp.int32, (1, width), 1)
        k = lax.rem(lane // rows_x, MZ)
        return jnp.where(k == 0, scale_zero, scale_rest).astype(F32)

    fwd_scale, inv_zero, inv_rest = zscales

    width = rows_x * nz_len

    def grid_half(grid, h):
        return grid[h * GC : (h + 1) * GC].reshape(half_rows, width)

    def whole(grid):
        return grid[...].reshape(chans * rows_y, width)

    def to_modes(grid, phase, h, scale):
        after_y = dot(y_fwd[...], grid_half(grid, h))
        rows = after_y.shape[0] // 2
        both = jnp.concatenate([after_y[:rows], after_y[rows:]], axis=1).astype(BF)
        out = (dot(both, z_fwd[...]) * scale).astype(BF)
        send_a[phase // 2, h] = out.reshape(peers, slab_half, lanes)

    def owned(phase, h, store):
        parts = []
        for s in range(gx):
            total = recv[phase, h, s * gy].astype(F32)
            for u in range(1, gy):
                total = total + recv[phase, h, s * gy + u].astype(F32)
            parts.append(total)
        values = split_dot(jnp.concatenate(parts, axis=1), x_fwd[...])
        for j in range(slab_half // GC):
            for r in range(2):
                store[r, h * GC : (h + 1) * GC, j * half_modes : (j + 1) * half_modes] = values[
                    j * GC : (j + 1) * GC, r * half_modes : (r + 1) * half_modes
                ]

    def to_slabs(store, phase, scale):
        rows = []
        for h in range(halves):
            for j in range(slab_half // GC):
                rows.append(
                    jnp.concatenate(
                        [
                            store[r, h * GC : (h + 1) * GC, j * half_modes : (j + 1) * half_modes]
                            for r in range(2)
                        ],
                        axis=1,
                    )
                )
        values = jnp.concatenate(rows, axis=0).astype(BF)
        out = (dot(values, x_inv[...]) * scale).astype(BF)
        for s in range(gx):
            for h in range(halves):
                send_b[phase // 2, h, s] = out[
                    h * slab_half : (h + 1) * slab_half, s * lanes : (s + 1) * lanes
                ]

    def spread(matrix):
        n = chans * rows_y
        row = lax.broadcasted_iota(jnp.int32, (n, chans), 0) // rows_y
        pick = (row == lax.broadcasted_iota(jnp.int32, (n, chans), 1)).astype(BF)
        col = lax.broadcasted_iota(jnp.int32, (chans, n), 1) // rows_y
        pick_t = (col == lax.broadcasted_iota(jnp.int32, (chans, n), 0)).astype(BF)
        wide = dot(dot(pick, matrix).astype(BF), pick_t)
        diag = lax.rem(lax.broadcasted_iota(jnp.int32, (n, n), 0), rows_y) == lax.rem(
            lax.broadcasted_iota(jnp.int32, (n, n), 1), rows_y
        )
        return jnp.where(diag, wide, 0.0).astype(BF)

    loaded("field", "y_fwd", "z_fwd")
    for h in range(halves):
        to_modes(field, 0, h, fwd_scale)
    pl.semaphore_wait(barrier, peers - 1)
    for h in range(halves):
        send(0, h)
    loaded("point", "bias")
    mix_a[...] = spread(point[...].T)
    mix_b[...] = spread(point[...])
    local[...] = dot(mix_a[...], whole(field))

    loaded("x_fwd", "weight", "x_inv")
    half = half_modes
    mixed = {}
    for h in range(halves):
        receive(0, h)
        owned(0, h, spec)
        for j in range(slab_half // GC):
            span = slice(j * half, (j + 1) * half)
            mixed_r, mixed_i = mixed.get(j, (0.0, 0.0))
            for c in range(h * GC, (h + 1) * GC):
                w_r = weight[0, c, :, span].astype(F32)
                w_i = weight[1, c, :, span].astype(F32)
                s_r = spec[0, c : c + 1, span]
                s_i = spec[1, c : c + 1, span]
                mixed_r = mixed_r + (s_r * w_r - s_i * w_i)
                mixed_i = mixed_i + (s_i * w_r + s_r * w_i)
            mixed[j] = (mixed_r, mixed_i)
    for j in range(slab_half // GC):
        span = slice(j * half, (j + 1) * half)
        grad[0, :, span] = mixed[j][0]
        grad[1, :, span] = mixed[j][1]
    to_slabs(grad, 1, zweight(gx * lanes, inv_zero, inv_rest))
    for h in range(halves):
        send(1, h)
    drain(0)

    loaded("z_inv", "y_inv", "cot")
    a = math.sqrt(2.0 / math.pi)
    for h in range(halves):
        rows = slice(h * half_rows, (h + 1) * half_rows)
        receive(1, h)
        pre_half = to_grid(recv[1, h], z_inv[...], y_inv[...]) + local[rows, :]
        for c in range(GC):
            o = h * GC + c
            pre = pre_half[c * rows_y : (c + 1) * rows_y] + bias[o]
            square = pre * pre
            t = jnp.tanh(a * pre * (1.0 + 0.044715 * square))
            cdf = 0.5 * (1.0 + t)
            out = (pre * cdf).astype(BF)
            slope = cdf + 0.5 * pre * (1.0 - t * t) * (a * (1.0 + 3.0 * 0.044715 * square))
            layer_out[o] = out
            grid_g[o] = (cot[o].astype(F32) * slope).astype(BF)
        some = slice(h * GC, (h + 1) * GC)
        for target, source in by_x(layer_out_h.at[some], layer_out.at[some]):
            store(source, target)
        to_modes(grid_g, 2, h, zweight(lanes, inv_zero, inv_rest))
        send(2, h)
    drain(1)
    local[...] = dot(mix_b[...], whole(grid_g))
    store(local, local_h)

    for h in range(halves):
        receive(2, h)
        owned(2, h, grad)
    for j in range(slab_half // GC):
        span = slice(j * half, (j + 1) * half)
        g_r = grad[0, :, span]
        g_i = grad[1, :, span]
        for c in range(chans):
            w_r = weight[0, c, :, span].astype(F32)
            w_i = weight[1, c, :, span].astype(F32)
            mode_grad[0, c : c + 1, span] = jnp.sum(w_r * g_r + w_i * g_i, axis=0, keepdims=True)
            mode_grad[1, c : c + 1, span] = jnp.sum(w_r * g_i - w_i * g_r, axis=0, keepdims=True)
    to_slabs(mode_grad, 3, fwd_scale)
    for h in range(halves):
        send(3, h)
    drain(2)
    store(spec, spec_h)
    store(grad, grad_h)
    for h in range(halves):
        receive(3, h)
        store(recv.at[3, h], modes_h.at[h])
    drain(3)
    for copy in stores:
        copy.wait()


def to_grid(modes, z_table, y_table):
    peers, slab_half, lanes = modes.shape
    after_z = dot(modes.reshape(peers * slab_half, lanes), z_table).astype(BF)
    width = after_z.shape[1] // 2
    both = jnp.concatenate([after_z[:, :width], after_z[:, width:]], axis=0)
    return dot(y_table, both)


def results(
    wg_scale, first_h, spec_h, grad_h, modes_h, local_h, z_inv_h, y_inv_h,
    layer_out_h, field_grad_h, weight_grad_h,
    first, spec, grad, modes, local, z_inv, y_inv, field_grad, weight_grad, sem,
):
    chans, rows_x, rows_y, nz_len = layer_out_h.shape
    half_rows = GC * rows_y

    def copy(source, target):
        copies.append(pltpu.make_async_copy(source, target, sem.at[len(copies)]))
        copies[-1].start()

    copies = []
    copy(spec_h, spec)
    copy(grad_h, grad)
    copy(modes_h, modes)
    copy(z_inv_h, z_inv)
    copy(y_inv_h.at[lax.axis_index("gy")], y_inv)
    copy(first_h, first)
    copy(local_h, local)
    copies[0].wait()
    copies[1].wait()
    quarter = chans // 4
    for q in range(4):
        some = slice(q * quarter, (q + 1) * quarter)
        for c in range(q * quarter, (q + 1) * quarter):
            s_r, s_i = spec[0, c : c + 1, :] * wg_scale, spec[1, c : c + 1, :] * wg_scale
            weight_grad[0, c] = grad[0] * s_r + grad[1] * s_i
            weight_grad[1, c] = grad[1] * s_r - grad[0] * s_i
        copy(weight_grad.at[:, some], weight_grad_h.at[:, some])
    copies[5].wait()
    copy(first, layer_out_h)
    for n in (2, 3, 4, 6):
        copies[n].wait()
    for h in range(modes.shape[0]):
        some = slice(h * GC, (h + 1) * GC)
        total = to_grid(modes[h], z_inv[...], y_inv[...]) + local[h * half_rows : (h + 1) * half_rows, :]
        field_grad[some] = total.astype(BF).reshape(GC, rows_y, rows_x * nz_len)
        for x in range(rows_x):
            copy(field_grad.at[some, :, x * nz_len : (x + 1) * nz_len], field_grad_h.at[some, x])
    for started in copies[7:]:
        started.wait()


def on_device_fused(gx, gy, field, cotangent, spectral_weight, point_weight, bias):
    chans, rows_x, rows_y, nz_len = field.shape
    peers = gx * gy
    owned_modes = spectral_weight.shape[3]
    total_cells = gx * gy * rows_x * rows_y * nz_len
    mode_count = MX * MY * MZ
    inv = 1.0 / math.sqrt(2.0 * mode_count)
    zscales = (1.0 / math.sqrt(total_cells), inv, 2.0 * inv)
    wg_scale = math.sqrt(2.0 * mode_count / total_cells)
    tables = [jnp.asarray(t) for t in constant_tables(gx, gy, rows_x, rows_y, nz_len)]
    y_fwd, y_inv, z_fwd, z_inv, x_fwd, x_inv = tables
    halves = chans // GC
    slab_half = MY // peers * GC
    lanes = 2 * MZ * rows_x
    rows, width = chans * rows_y, rows_x * nz_len
    hbm = pl.BlockSpec(memory_space=pltpu.HBM)
    grid = pltpu.VMEM((chans, rows_y, width), BF)
    modes = pltpu.VMEM((2, chans, owned_modes), F32)

    def body(*refs):
        fused(gx, gy, zscales, *refs)

    layer_out, spec, grad, grad_modes, local = pl.pallas_call(
        body,
        out_shape=(
            jax.ShapeDtypeStruct(field.shape, BF),
            jax.ShapeDtypeStruct(modes.shape, F32),
            jax.ShapeDtypeStruct(modes.shape, F32),
            jax.ShapeDtypeStruct((halves, peers, slab_half, lanes), BF),
            jax.ShapeDtypeStruct((rows, width), F32),
        ),
        in_specs=[hbm] * 11,
        out_specs=(hbm,) * 5,
        scratch_shapes=[
            grid,
            grid,
            pltpu.VMEM(spectral_weight.shape, BF),
            pltpu.VMEM(point_weight.shape, BF),
            pltpu.SMEM(bias.shape, F32),
            pltpu.VMEM(y_fwd.shape[1:], BF),
            pltpu.VMEM(z_fwd.shape, BF),
            pltpu.VMEM(z_inv.shape, BF),
            pltpu.VMEM(y_inv.shape[1:], BF),
            pltpu.VMEM(x_fwd.shape, BF),
            pltpu.VMEM(x_inv.shape, BF),
            grid,
            pltpu.VMEM((2, halves, peers, slab_half, lanes), BF),
            pltpu.VMEM((2, halves, gx, slab_half, lanes), BF),
            pltpu.VMEM((4, halves, peers, slab_half, lanes), BF),
            grid,
            pltpu.VMEM((rows, width), F32),
            modes,
            modes,
            modes,
            pltpu.VMEM((rows, rows), BF),
            pltpu.VMEM((rows, rows), BF),
            pltpu.SemaphoreType.DMA((4, halves)),
            pltpu.SemaphoreType.DMA((4, halves)),
            pltpu.SemaphoreType.DMA((2 * rows_x + 9,)),
            pltpu.SemaphoreType.DMA((halves * (rows_x + 1) + 3,)),
        ],
        compiler_params=pltpu.CompilerParams(
            collective_id=0, has_side_effects=True, vmem_limit_bytes=56 * 1024 * 1024
        ),
    )(field, cotangent, spectral_weight, point_weight, bias, y_fwd, z_fwd, z_inv, y_inv, x_fwd, x_inv)
    return pl.pallas_call(
        functools.partial(results, wg_scale),
        out_shape=(
            jax.ShapeDtypeStruct(field.shape, BF),
            jax.ShapeDtypeStruct(field.shape, BF),
            jax.ShapeDtypeStruct(spectral_weight.shape, F32),
        ),
        in_specs=[hbm] * 7,
        out_specs=(hbm, hbm, hbm),
        scratch_shapes=[
            pltpu.VMEM(field.shape, BF),
            modes,
            modes,
            pltpu.VMEM(grad_modes.shape, BF),
            pltpu.VMEM(local.shape, F32),
            pltpu.VMEM(z_inv.shape, BF),
            pltpu.VMEM(y_inv.shape[1:], BF),
            grid,
            pltpu.VMEM(spectral_weight.shape, F32),
            pltpu.SemaphoreType.DMA((12 + halves * rows_x,)),
        ],
        compiler_params=pltpu.CompilerParams(vmem_limit_bytes=56 * 1024 * 1024),
    )(layer_out, spec, grad, grad_modes, local, z_inv, y_inv)


def solution(mesh):
    gx, gy = mesh.shape["gx"], mesh.shape["gy"]
    in_specs = (
        P(None, ("groups", "gx"), "gy", None),
        P(None, ("groups", "gx"), "gy", None),
        P(None, None, None, ("gx", "gy")),
        P(),
        P(),
    )
    out_specs = (
        P(None, ("groups", "gx"), "gy", None),
        P(None, ("groups", "gx"), "gy", None),
        P("groups", None, None, ("gx", "gy")),
    )

    def local_program(field, cotangent, spectral_weight, point_weight, bias):
        rows_x = field.shape[1]
        fits = MY % (gx * gy) == 0 and MY // (gx * gy) * GC % 16 == 0
        fits = fits and 2 * MZ * rows_x == 128 and field.shape[0] % GC == 0
        if fits:
            return on_device_fused(gx, gy, field, cotangent, spectral_weight, point_weight, bias)
        return on_device(field, cotangent, spectral_weight, point_weight, bias)

    return jax.shard_map(
        local_program, mesh=mesh, in_specs=in_specs, out_specs=out_specs, check_vma=False
    )
```

```python
import functools
import math

import jax
import jax.numpy as jnp
import numpy as np
from jax import lax
from jax.experimental import pallas as pl
from jax.experimental.pallas import tpu as pltpu
from jax.sharding import PartitionSpec as P

MX = 32
MY = 32
MZ = 16


def phase_tables(count, length, offset, rows, signed):
    position = offset + jnp.arange(rows, dtype=jnp.int32)
    freq = jnp.arange(count, dtype=jnp.int32)
    if signed:
        freq = jnp.where(freq >= count // 2, freq + (length - count), freq)
    turns = freq[:, None] * position[None, :] % length
    angle = turns.astype(jnp.float32) * (2.0 * math.pi / length)
    return (jnp.cos(angle).astype(jnp.bfloat16), jnp.sin(angle).astype(jnp.bfloat16))


def z_transform(block, cos_z, sin_z):
    chans, rows_x, rows_y, nz_len = block.shape
    kept = cos_z.shape[0]
    tables = jnp.concatenate([cos_z, sin_z], axis=0)
    flat = jnp.dot(block.reshape(-1, nz_len), tables.T, preferred_element_type=jnp.float32)
    flat = flat.reshape(chans, rows_x, rows_y, 2 * kept)
    both = jnp.transpose(flat, (0, 3, 1, 2))
    return (both[:, :kept], both[:, kept:])


def point_mix(matrix, grid):
    chans = grid.shape[0]
    flat = jnp.dot(matrix, grid.reshape(chans, -1), preferred_element_type=jnp.float32)
    return flat.reshape(grid.shape)


def forward_yz(block, y_start, zscale, ny_total):
    hp = lax.Precision.HIGHEST
    rows_y = block.shape[2]
    nz_len = block.shape[3]
    cos_z, sin_z = phase_tables(MZ, nz_len, 0, nz_len, False)
    zscale_b = zscale[None, :, None, None]
    z_cos, z_sin = z_transform(block, cos_z, sin_z)
    part_r = z_cos * zscale_b
    part_i = -z_sin * zscale_b
    cos_y, sin_y = phase_tables(MY, ny_total, y_start, rows_y, True)
    cos_y = cos_y.astype(jnp.float32)
    sin_y = sin_y.astype(jnp.float32)
    out_r = jnp.einsum("ckxy,jy->cjkx", part_r, cos_y, precision=hp) + jnp.einsum(
        "ckxy,jy->cjkx", part_i, sin_y, precision=hp
    )
    out_i = jnp.einsum("ckxy,jy->cjkx", part_i, cos_y, precision=hp) - jnp.einsum(
        "ckxy,jy->cjkx", part_r, sin_y, precision=hp
    )
    return (out_r, out_i)


def forward_x(part_r, part_i, x_start, nx_total):
    hp = lax.Precision.HIGHEST
    chans = part_r.shape[0]
    rows_x = part_r.shape[3]
    cos_x, sin_x = phase_tables(MX, nx_total, x_start, rows_x, True)
    cos_x = cos_x.astype(jnp.float32)
    sin_x = sin_x.astype(jnp.float32)
    out_r = jnp.einsum("cjkx,ix->cjki", part_r, cos_x, precision=hp) + jnp.einsum(
        "cjkx,ix->cjki", part_i, sin_x, precision=hp
    )
    out_i = jnp.einsum("cjkx,ix->cjki", part_i, cos_x, precision=hp) - jnp.einsum(
        "cjkx,ix->cjki", part_r, sin_x, precision=hp
    )
    return jnp.stack([out_r.reshape(chans, -1), out_i.reshape(chans, -1)])


def inverse_modes(modes, x_start, y_start, zweight, nx_total, ny_total, rows_x, rows_y, nz_len):
    hp = lax.Precision.HIGHEST
    chans = modes.shape[1]
    values = modes.astype(jnp.float32).reshape(2, chans, MY, MZ, MX)
    mode_r = values[0]
    mode_i = values[1]
    cos_x, sin_x = phase_tables(MX, nx_total, x_start, rows_x, True)
    cos_x = cos_x.astype(jnp.float32)
    sin_x = sin_x.astype(jnp.float32)
    step_r = jnp.einsum("cjki,ix->cxjk", mode_r, cos_x, precision=hp) - jnp.einsum(
        "cjki,ix->cxjk", mode_i, sin_x, precision=hp
    )
    step_i = jnp.einsum("cjki,ix->cxjk", mode_i, cos_x, precision=hp) + jnp.einsum(
        "cjki,ix->cxjk", mode_r, sin_x, precision=hp
    )
    cos_y, sin_y = phase_tables(MY, ny_total, y_start, rows_y, True)
    cos_y = cos_y.astype(jnp.float32)
    sin_y = sin_y.astype(jnp.float32)
    next_r = jnp.einsum("cxjk,jy->cxyk", step_r, cos_y, precision=hp) - jnp.einsum(
        "cxjk,jy->cxyk", step_i, sin_y, precision=hp
    )
    next_i = jnp.einsum("cxjk,jy->cxyk", step_i, cos_y, precision=hp) + jnp.einsum(
        "cxjk,jy->cxyk", step_r, sin_y, precision=hp
    )
    cos_z, sin_z = phase_tables(MZ, nz_len, 0, nz_len, False)
    cos_z = cos_z.astype(jnp.float32)
    sin_z = sin_z.astype(jnp.float32)
    next_r = next_r * zweight
    next_i = next_i * zweight
    return jnp.einsum("cxyk,kz->cxyz", next_r, cos_z, precision=hp) - jnp.einsum(
        "cxyk,kz->cxyz", next_i, sin_z, precision=hp
    )


def channel_mix(spectrum, weight):
    hp = lax.Precision.HIGHEST
    w_r = weight[0].astype(jnp.float32)
    w_i = weight[1].astype(jnp.float32)
    out_r = jnp.einsum("im,iom->om", spectrum[0], w_r, precision=hp) - jnp.einsum(
        "im,iom->om", spectrum[1], w_i, precision=hp
    )
    out_i = jnp.einsum("im,iom->om", spectrum[1], w_r, precision=hp) + jnp.einsum(
        "im,iom->om", spectrum[0], w_i, precision=hp
    )
    return jnp.stack([out_r, out_i])


def mix_grads(spectrum, mixed_grad, weight):
    hp = lax.Precision.HIGHEST
    w_r = weight[0].astype(jnp.float32)
    w_i = weight[1].astype(jnp.float32)
    grad_r = jnp.einsum("om,im->iom", mixed_grad[0], spectrum[0], precision=hp) + jnp.einsum(
        "om,im->iom", mixed_grad[1], spectrum[1], precision=hp
    )
    grad_i = jnp.einsum("om,im->iom", mixed_grad[1], spectrum[0], precision=hp) - jnp.einsum(
        "om,im->iom", mixed_grad[0], spectrum[1], precision=hp
    )
    back_r = jnp.einsum("iom,om->im", w_r, mixed_grad[0], precision=hp) + jnp.einsum(
        "iom,om->im", w_i, mixed_grad[1], precision=hp
    )
    back_i = jnp.einsum("iom,om->im", w_r, mixed_grad[1], precision=hp) - jnp.einsum(
        "iom,om->im", w_i, mixed_grad[0], precision=hp
    )
    return (jnp.stack([grad_r, grad_i]), jnp.stack([back_r, back_i]))


def owned_spectrum(block, x_start, y_start, zscale, nx_total, ny_total):
    part_r, part_i = forward_yz(block, y_start, zscale, ny_total)
    whole = forward_x(part_r, part_i, x_start, nx_total)
    return lax.psum_scatter(whole, ("gx", "gy"), scatter_dimension=2, tiled=True)


def all_modes(owned_block):
    return lax.all_gather(owned_block, ("gx", "gy"), axis=2, tiled=True)


def on_device(field, cotangent, spectral_weight, point_weight, bias):
    rows_x = field.shape[1]
    rows_y = field.shape[2]
    nz_len = field.shape[3]
    nx_total = rows_x * lax.axis_size("gx")
    ny_total = rows_y * lax.axis_size("gy")
    total_cells = nx_total * ny_total * nz_len
    mode_count = MX * MY * MZ
    x_start = lax.axis_index("gx") * rows_x
    y_start = lax.axis_index("gy") * rows_y
    zindex = jnp.arange(MZ, dtype=jnp.int32)
    forward_scale = jnp.full((MZ,), 1.0 / math.sqrt(total_cells), jnp.float32)
    inverse_scale = jnp.where(zindex == 0, 1.0, 2.0).astype(jnp.float32) / math.sqrt(
        2.0 * mode_count
    )
    spectrum = owned_spectrum(field, x_start, y_start, forward_scale, nx_total, ny_total)
    mixed = channel_mix(spectrum, spectral_weight).astype(jnp.bfloat16)
    mixed_all = all_modes(mixed)
    spectral_out = inverse_modes(
        mixed_all, x_start, y_start, inverse_scale, nx_total, ny_total, rows_x, rows_y, nz_len
    )
    pre = spectral_out + point_mix(point_weight.T, field) + bias[:, None, None, None]
    layer_out = jax.nn.gelu(pre).astype(jnp.bfloat16)
    pre_grad = jax.vjp(jax.nn.gelu, pre)[1](cotangent.astype(jnp.float32))[0].astype(jnp.bfloat16)
    mixed_grad = owned_spectrum(pre_grad, x_start, y_start, inverse_scale, nx_total, ny_total)
    weight_grad, spectrum_grad = mix_grads(spectrum, mixed_grad, spectral_weight)
    weight_grad = weight_grad * math.sqrt(2.0 * mode_count / total_cells)
    grad_all = all_modes(spectrum_grad.astype(jnp.bfloat16))
    local = point_mix(point_weight, pre_grad)
    spectral = inverse_modes(
        grad_all, x_start, y_start, forward_scale, nx_total, ny_total, rows_x, rows_y, nz_len
    )
    field_grad = (local + spectral).astype(jnp.bfloat16)
    return (layer_out, field_grad, weight_grad)


BF = jnp.bfloat16
F32 = jnp.float32
MESH = pl.DeviceIdType.MESH
GC = 8


def host_tables(count, length, cells, signed):
    freq = np.arange(count)
    if signed:
        freq = np.where(freq >= count // 2, freq + (length - count), freq)
    turns = (freq[:, None] * cells[None, :]) % length
    angle = turns.astype(np.float32) * np.float32(2.0 * math.pi / length)
    rounded = [np.asarray(fn(angle)).astype(BF).astype(np.float32) for fn in (np.cos, np.sin)]
    return rounded[0], rounded[1]


def constant_tables(gx, gy, rows_x, rows_y, nz_len):
    nx_total, ny_total = rows_x * gx, rows_y * gy
    cos_x, sin_x = host_tables(MX, nx_total, np.arange(nx_total), True)
    cos_y, sin_y = host_tables(MY, ny_total, np.arange(ny_total), True)
    cos_z, sin_z = host_tables(MZ, nz_len, np.arange(nz_len), False)
    eye_c, eye_x, eye_k = np.eye(GC), np.eye(rows_x), np.eye(MZ)
    cy = cos_y.reshape(MY, gy, rows_y)
    sy = sin_y.reshape(MY, gy, rows_y)
    y_fwd = np.stack([np.einsum("jgy,cd->gjcdy", t, eye_c) for t in (cy, sy)], axis=1)
    y_fwd = y_fwd.reshape(gy, 2 * MY * GC, GC * rows_y)
    y_inv = np.stack([np.einsum("jgy,cd->gcyjd", t, eye_c) for t in (cy, -sy)], axis=3)
    y_inv = y_inv.reshape(gy, GC * rows_y, 2 * MY * GC)
    z_pairs = np.stack([np.stack([cos_z, -sin_z]), np.stack([-sin_z, -cos_z])])
    z_fwd = np.einsum("arkz,xw->axzrkw", z_pairs, eye_x)
    z_fwd = z_fwd.reshape(2 * rows_x * nz_len, 2 * MZ * rows_x)
    i_pairs = np.stack([np.stack([cos_z, -sin_z]), np.stack([sin_z, cos_z])])
    z_inv = np.einsum("arkz,xw->rkwaxz", i_pairs, eye_x)
    z_inv = z_inv.reshape(2 * MZ * rows_x, 2 * rows_x * nz_len)
    x_pairs = np.stack([np.stack([cos_x, -sin_x]), np.stack([sin_x, cos_x])])
    x_pairs = x_pairs.reshape(2, 2, MX, gx, rows_x)
    x_fwd = np.einsum("rsigx,kl->grkxsli", x_pairs, eye_k)
    x_fwd = x_fwd.reshape(gx * 2 * MZ * rows_x, 2 * MZ * MX)
    x_inv = np.ascontiguousarray(x_fwd.T)
    return [t.astype(BF) for t in (y_fwd, y_inv, z_fwd, z_inv, x_fwd, x_inv)]


def dot(a, b):
    return jnp.dot(a, b, preferred_element_type=F32)


def split_dot(a, b):
    high = a.astype(BF)
    low = (a - high.astype(F32)).astype(BF)
    both = dot(jnp.concatenate([high, low], axis=0), b)
    return both[: a.shape[0]] + both[a.shape[0] :]


def fused(
    gx, gy, zscales,
    field_h, cot_h, weight_h, point_h, bias_h, y_fwd_h, z_fwd_h, z_inv_h, y_inv_h, x_fwd_h, x_inv_h,
    layer_out_h, spec_h, grad_h, modes_h, local_h,
    field, cot, weight, point, bias, y_fwd, z_fwd, z_inv, y_inv, x_fwd, x_inv, layer_out,
    send_a, send_b, recv, grid_g, local, spec, grad, mode_grad, mix_a, mix_b, send_sem, recv_sem,
    load_sem, store_sem,
):
    peers = gx * gy
    chans, rows_x, rows_y, nz_len = field_h.shape
    half_rows = GC * rows_y
    halves = chans // GC
    slab_half, lanes = recv.shape[3:]
    me_x, me_y = lax.axis_index("gx"), lax.axis_index("gy")
    me = me_x * gy + me_y
    half_modes = MZ * MX

    def peer(step):
        down = peers - 1 - step
        down = down - (down <= me).astype(jnp.int32)
        up = step + (step >= me).astype(jnp.int32)
        other = jnp.where(me < peers // 2, down, up)
        return other, {"gx": other // gy, "gy": lax.rem(other, gy)}

    barrier = pltpu.get_barrier_semaphore()
    loads = {}
    stores = []

    def store(source, target):
        stores.append(pltpu.make_async_copy(source, target, store_sem.at[len(stores)]))
        stores[-1].start()


    def load(name, *pairs):
        copies = []
        for source, target in pairs:
            count = sum(len(c) for c in loads.values()) + len(copies)
            copies.append(pltpu.make_async_copy(source, target, load_sem.at[count]))
            copies[-1].start()
        loads[name] = copies

    def loaded(*names):
        for name in names:
            for copy in loads[name]:
                copy.wait()

    def by_x(flat, grid):
        return [
            (flat.at[:, x], grid.at[:, :, x * nz_len : (x + 1) * nz_len]) for x in range(rows_x)
        ]

    load("field", *by_x(field_h, field))
    load("y_fwd", (y_fwd_h.at[me_y], y_fwd))
    load("z_fwd", (z_fwd_h, z_fwd))
    load("point", (point_h, point))
    load("bias", (bias_h, bias))
    load("x_fwd", (x_fwd_h, x_fwd))
    load("weight", (weight_h, weight))
    load("x_inv", (x_inv_h, x_inv))
    load("z_inv", (z_inv_h, z_inv))
    load("y_inv", (y_inv_h.at[me_y], y_inv))
    load("cot", *by_x(cot_h, cot))

    def greet(step, carry):
        pl.semaphore_signal(barrier, inc=1, device_id=peer(step)[1], device_id_type=MESH)
        return carry

    lax.fori_loop(0, peers - 1, greet, 0, unroll=True)

    def copy_to(phase, h, step):
        other, where = peer(step)
        buffer = send_a.at[phase // 2, h, other] if phase % 2 == 0 else send_b.at[phase // 2, h, other // gy]
        return pltpu.make_async_remote_copy(
            src_ref=buffer,
            dst_ref=recv.at[phase, h, me],
            send_sem=send_sem.at[phase, h],
            recv_sem=recv_sem.at[phase, h],
            device_id=where,
            device_id_type=MESH,
        )

    def send(phase, h):
        def one(step, carry):
            copy_to(phase, h, step).start()
            return carry

        lax.fori_loop(0, peers - 1, one, 0, unroll=True)
        if phase % 2 == 0:
            recv[phase, h, me] = send_a[phase // 2, h, me]
        else:
            recv[phase, h, me] = send_b[phase // 2, h, me_x]

    def all_slabs(phase, h):
        slabs = recv.at[phase, h, pl.ds(0, peers - 1)]
        return pltpu.make_async_remote_copy(
            src_ref=slabs,
            dst_ref=slabs,
            send_sem=send_sem.at[phase, h],
            recv_sem=recv_sem.at[phase, h],
            device_id=peer(0)[1],
            device_id_type=MESH,
        )

    def receive(phase, h):
        all_slabs(phase, h).wait_recv()

    def drain(phase):
        for h in range(halves):
            all_slabs(phase, h).wait_send()

    def last_copy(step):
        other, where = peer(step)
        return pltpu.make_async_remote_copy(
            src_ref=send_b.at[1, :, other // gy],
            dst_ref=recv.at[3, :, me],
            send_sem=send_sem.at[3, 0],
            recv_sem=recv_sem.at[3, 0],
            device_id=where,
            device_id_type=MESH,
        )

    def zweight(width, scale_zero, scale_rest):
        lane = lax.broadcasted_iota(jnp.int32, (1, width), 1)
        k = lax.rem(lane // rows_x, MZ)
        return jnp.where(k == 0, scale_zero, scale_rest).astype(F32)

    fwd_scale, inv_zero, inv_rest = zscales

    width = rows_x * nz_len

    def grid_half(grid, h):
        return grid[h * GC : (h + 1) * GC].reshape(half_rows, width)

    def whole(grid):
        return grid[...].reshape(chans * rows_y, width)

    def to_modes(grid, phase, h, scale):
        after_y = dot(y_fwd[...], grid_half(grid, h))
        rows = after_y.shape[0] // 2
        both = jnp.concatenate([after_y[:rows], after_y[rows:]], axis=1).astype(BF)
        out = (dot(both, z_fwd[...]) * scale).astype(BF)
        send_a[phase // 2, h] = out.reshape(peers, slab_half, lanes)

    def owned(phase, h, store):
        parts = []
        for s in range(gx):
            total = recv[phase, h, s * gy].astype(F32)
            for u in range(1, gy):
                total = total + recv[phase, h, s * gy + u].astype(F32)
            parts.append(total)
        values = split_dot(jnp.concatenate(parts, axis=1), x_fwd[...])
        for j in range(slab_half // GC):
            for r in range(2):
                store[r, h * GC : (h + 1) * GC, j * half_modes : (j + 1) * half_modes] = values[
                    j * GC : (j + 1) * GC, r * half_modes : (r + 1) * half_modes
                ]

    def to_slabs(store, phase, scale):
        rows = []
        for h in range(halves):
            for j in range(slab_half // GC):
                rows.append(
                    jnp.concatenate(
                        [
                            store[r, h * GC : (h + 1) * GC, j * half_modes : (j + 1) * half_modes]
                            for r in range(2)
                        ],
                        axis=1,
                    )
                )
        values = jnp.concatenate(rows, axis=0).astype(BF)
        out = (dot(values, x_inv[...]) * scale).astype(BF)
        for s in range(gx):
            for h in range(halves):
                send_b[phase // 2, h, s] = out[
                    h * slab_half : (h + 1) * slab_half, s * lanes : (s + 1) * lanes
                ]

    def spread(matrix):
        n = chans * rows_y
        row = lax.broadcasted_iota(jnp.int32, (n, chans), 0) // rows_y
        pick = (row == lax.broadcasted_iota(jnp.int32, (n, chans), 1)).astype(BF)
        col = lax.broadcasted_iota(jnp.int32, (chans, n), 1) // rows_y
        pick_t = (col == lax.broadcasted_iota(jnp.int32, (chans, n), 0)).astype(BF)
        wide = dot(dot(pick, matrix).astype(BF), pick_t)
        diag = lax.rem(lax.broadcasted_iota(jnp.int32, (n, n), 0), rows_y) == lax.rem(
            lax.broadcasted_iota(jnp.int32, (n, n), 1), rows_y
        )
        return jnp.where(diag, wide, 0.0).astype(BF)

    loaded("field", "y_fwd", "z_fwd")
    for h in range(halves):
        to_modes(field, 0, h, fwd_scale)
    pl.semaphore_wait(barrier, peers - 1)
    for h in range(halves):
        send(0, h)
    loaded("point", "bias")
    mix_a[...] = spread(point[...].T)
    mix_b[...] = spread(point[...])
    local[...] = dot(mix_a[...], whole(field))

    loaded("x_fwd", "weight", "x_inv")
    half = half_modes
    mixed = {}
    for h in range(halves):
        receive(0, h)
        owned(0, h, spec)
        for j in range(slab_half // GC):
            span = slice(j * half, (j + 1) * half)
            mixed_r, mixed_i = mixed.get(j, (0.0, 0.0))
            for c in range(h * GC, (h + 1) * GC):
                w_r = weight[0, c, :, span].astype(F32)
                w_i = weight[1, c, :, span].astype(F32)
                s_r = spec[0, c : c + 1, span]
                s_i = spec[1, c : c + 1, span]
                mixed_r = mixed_r + (s_r * w_r - s_i * w_i)
                mixed_i = mixed_i + (s_i * w_r + s_r * w_i)
            mixed[j] = (mixed_r, mixed_i)
    for j in range(slab_half // GC):
        span = slice(j * half, (j + 1) * half)
        grad[0, :, span] = mixed[j][0]
        grad[1, :, span] = mixed[j][1]
    to_slabs(grad, 1, zweight(gx * lanes, inv_zero, inv_rest))
    for h in range(halves):
        send(1, h)
    drain(0)

    loaded("z_inv", "y_inv", "cot")
    a = math.sqrt(2.0 / math.pi)
    for h in range(halves):
        rows = slice(h * half_rows, (h + 1) * half_rows)
        receive(1, h)
        pre_half = to_grid(recv[1, h], z_inv[...], y_inv[...]) + local[rows, :]
        for c in range(GC):
            o = h * GC + c
            pre = pre_half[c * rows_y : (c + 1) * rows_y] + bias[o]
            square = pre * pre
            t = jnp.tanh(a * pre * (1.0 + 0.044715 * square))
            cdf = 0.5 * (1.0 + t)
            out = (pre * cdf).astype(BF)
            slope = cdf + 0.5 * pre * (1.0 - t * t) * (a * (1.0 + 3.0 * 0.044715 * square))
            layer_out[o] = out
            grid_g[o] = (cot[o].astype(F32) * slope).astype(BF)
        some = slice(h * GC, (h + 1) * GC)
        for target, source in by_x(layer_out_h.at[some], layer_out.at[some]):
            store(source, target)
        to_modes(grid_g, 2, h, zweight(lanes, inv_zero, inv_rest))
        send(2, h)
    drain(1)
    local[...] = dot(mix_b[...], whole(grid_g))
    store(local, local_h)

    for h in range(halves):
        receive(2, h)
        owned(2, h, grad)
    for j in range(slab_half // GC):
        span = slice(j * half, (j + 1) * half)
        g_r = grad[0, :, span]
        g_i = grad[1, :, span]
        for c in range(chans):
            w_r = weight[0, c, :, span].astype(F32)
            w_i = weight[1, c, :, span].astype(F32)
            mode_grad[0, c : c + 1, span] = jnp.sum(w_r * g_r + w_i * g_i, axis=0, keepdims=True)
            mode_grad[1, c : c + 1, span] = jnp.sum(w_r * g_i - w_i * g_r, axis=0, keepdims=True)
    to_slabs(mode_grad, 3, fwd_scale)
    for step in range(peers - 1):
        last_copy(step).start()
    recv[3, :, me] = send_b[1, :, me_x]
    drain(2)
    store(spec, spec_h)
    store(grad, grad_h)
    slabs = recv.at[3, :, pl.ds(0, peers - 1)]
    whole_copy = pltpu.make_async_remote_copy(
        src_ref=slabs,
        dst_ref=slabs,
        send_sem=send_sem.at[3, 0],
        recv_sem=recv_sem.at[3, 0],
        device_id=peer(0)[1],
        device_id_type=MESH,
    )
    whole_copy.wait_recv()
    store(recv.at[3], modes_h)
    whole_copy.wait_send()
    for copy in stores:
        copy.wait()


def to_grid(modes, z_table, y_table):
    peers, slab_half, lanes = modes.shape
    after_z = dot(modes.reshape(peers * slab_half, lanes), z_table).astype(BF)
    width = after_z.shape[1] // 2
    both = jnp.concatenate([after_z[:, :width], after_z[:, width:]], axis=0)
    return dot(y_table, both)


def results(
    wg_scale, first_h, spec_h, grad_h, modes_h, local_h, z_inv_h, y_inv_h,
    layer_out_h, field_grad_h, weight_grad_h,
    first, spec, grad, modes, local, z_inv, y_inv, field_grad, weight_grad, sem,
):
    chans, rows_x, rows_y, nz_len = layer_out_h.shape
    half_rows = GC * rows_y

    def copy(source, target):
        copies.append(pltpu.make_async_copy(source, target, sem.at[len(copies)]))
        copies[-1].start()

    copies = []
    copy(spec_h, spec)
    copy(grad_h, grad)
    copy(modes_h, modes)
    copy(z_inv_h, z_inv)
    copy(y_inv_h.at[lax.axis_index("gy")], y_inv)
    copy(first_h, first)
    copy(local_h, local)
    copies[0].wait()
    copies[1].wait()
    quarter = chans // 4
    for q in range(4):
        some = slice(q * quarter, (q + 1) * quarter)
        for c in range(q * quarter, (q + 1) * quarter):
            s_r, s_i = spec[0, c : c + 1, :] * wg_scale, spec[1, c : c + 1, :] * wg_scale
            weight_grad[0, c] = grad[0] * s_r + grad[1] * s_i
            weight_grad[1, c] = grad[1] * s_r - grad[0] * s_i
        copy(weight_grad.at[:, some], weight_grad_h.at[:, some])
    copies[5].wait()
    copy(first, layer_out_h)
    for n in (2, 3, 4, 6):
        copies[n].wait()
    for h in range(modes.shape[0]):
        some = slice(h * GC, (h + 1) * GC)
        total = to_grid(modes[h], z_inv[...], y_inv[...]) + local[h * half_rows : (h + 1) * half_rows, :]
        field_grad[some] = total.astype(BF).reshape(GC, rows_y, rows_x * nz_len)
        for x in range(rows_x):
            copy(field_grad.at[some, :, x * nz_len : (x + 1) * nz_len], field_grad_h.at[some, x])
    for started in copies[7:]:
        started.wait()


def on_device_fused(gx, gy, field, cotangent, spectral_weight, point_weight, bias):
    chans, rows_x, rows_y, nz_len = field.shape
    peers = gx * gy
    owned_modes = spectral_weight.shape[3]
    total_cells = gx * gy * rows_x * rows_y * nz_len
    mode_count = MX * MY * MZ
    inv = 1.0 / math.sqrt(2.0 * mode_count)
    zscales = (1.0 / math.sqrt(total_cells), inv, 2.0 * inv)
    wg_scale = math.sqrt(2.0 * mode_count / total_cells)
    tables = [jnp.asarray(t) for t in constant_tables(gx, gy, rows_x, rows_y, nz_len)]
    y_fwd, y_inv, z_fwd, z_inv, x_fwd, x_inv = tables
    halves = chans // GC
    slab_half = MY // peers * GC
    lanes = 2 * MZ * rows_x
    rows, width = chans * rows_y, rows_x * nz_len
    hbm = pl.BlockSpec(memory_space=pltpu.HBM)
    grid = pltpu.VMEM((chans, rows_y, width), BF)
    modes = pltpu.VMEM((2, chans, owned_modes), F32)

    def body(*refs):
        fused(gx, gy, zscales, *refs)

    layer_out, spec, grad, grad_modes, local = pl.pallas_call(
        body,
        out_shape=(
            jax.ShapeDtypeStruct(field.shape, BF),
            jax.ShapeDtypeStruct(modes.shape, F32),
            jax.ShapeDtypeStruct(modes.shape, F32),
            jax.ShapeDtypeStruct((halves, peers, slab_half, lanes), BF),
            jax.ShapeDtypeStruct((rows, width), F32),
        ),
        in_specs=[hbm] * 11,
        out_specs=(hbm,) * 5,
        scratch_shapes=[
            grid,
            grid,
            pltpu.VMEM(spectral_weight.shape, BF),
            pltpu.VMEM(point_weight.shape, BF),
            pltpu.SMEM(bias.shape, F32),
            pltpu.VMEM(y_fwd.shape[1:], BF),
            pltpu.VMEM(z_fwd.shape, BF),
            pltpu.VMEM(z_inv.shape, BF),
            pltpu.VMEM(y_inv.shape[1:], BF),
            pltpu.VMEM(x_fwd.shape, BF),
            pltpu.VMEM(x_inv.shape, BF),
            grid,
            pltpu.VMEM((2, halves, peers, slab_half, lanes), BF),
            pltpu.VMEM((2, halves, gx, slab_half, lanes), BF),
            pltpu.VMEM((4, halves, peers, slab_half, lanes), BF),
            grid,
            pltpu.VMEM((rows, width), F32),
            modes,
            modes,
            modes,
            pltpu.VMEM((rows, rows), BF),
            pltpu.VMEM((rows, rows), BF),
            pltpu.SemaphoreType.DMA((4, halves)),
            pltpu.SemaphoreType.DMA((4, halves)),
            pltpu.SemaphoreType.DMA((2 * rows_x + 9,)),
            pltpu.SemaphoreType.DMA((halves * (rows_x + 1) + 3,)),
        ],
        compiler_params=pltpu.CompilerParams(
            collective_id=0, has_side_effects=True, vmem_limit_bytes=56 * 1024 * 1024
        ),
    )(field, cotangent, spectral_weight, point_weight, bias, y_fwd, z_fwd, z_inv, y_inv, x_fwd, x_inv)
    return pl.pallas_call(
        functools.partial(results, wg_scale),
        out_shape=(
            jax.ShapeDtypeStruct(field.shape, BF),
            jax.ShapeDtypeStruct(field.shape, BF),
            jax.ShapeDtypeStruct(spectral_weight.shape, F32),
        ),
        in_specs=[hbm] * 7,
        out_specs=(hbm, hbm, hbm),
        scratch_shapes=[
            pltpu.VMEM(field.shape, BF),
            modes,
            modes,
            pltpu.VMEM(grad_modes.shape, BF),
            pltpu.VMEM(local.shape, F32),
            pltpu.VMEM(z_inv.shape, BF),
            pltpu.VMEM(y_inv.shape[1:], BF),
            grid,
            pltpu.VMEM(spectral_weight.shape, F32),
            pltpu.SemaphoreType.DMA((12 + halves * rows_x,)),
        ],
        compiler_params=pltpu.CompilerParams(vmem_limit_bytes=56 * 1024 * 1024),
    )(layer_out, spec, grad, grad_modes, local, z_inv, y_inv)


def solution(mesh):
    gx, gy = mesh.shape["gx"], mesh.shape["gy"]
    in_specs = (
        P(None, ("groups", "gx"), "gy", None),
        P(None, ("groups", "gx"), "gy", None),
        P(None, None, None, ("gx", "gy")),
        P(),
        P(),
    )
    out_specs = (
        P(None, ("groups", "gx"), "gy", None),
        P(None, ("groups", "gx"), "gy", None),
        P("groups", None, None, ("gx", "gy")),
    )

    def local_program(field, cotangent, spectral_weight, point_weight, bias):
        rows_x = field.shape[1]
        fits = MY % (gx * gy) == 0 and MY // (gx * gy) * GC % 16 == 0
        fits = fits and 2 * MZ * rows_x == 128 and field.shape[0] % GC == 0
        if fits:
            return on_device_fused(gx, gy, field, cotangent, spectral_weight, point_weight, bias)
        return on_device(field, cotangent, spectral_weight, point_weight, bias)

    return jax.shard_map(
        local_program, mesh=mesh, in_specs=in_specs, out_specs=out_specs, check_vma=False
    )
```
